256 devices in a mesh: fsdp: 64 (over z, y, core), rep: 4 (over x).
Axes of the slice: x: 4, y: 4, z: 8, core: 2. Of those that a mesh axis runs over, the one named last changes fastest.
Arguments:
- grad: float32 [4096, 12288], P('fsdp'), may hold values from -6 to 6
- left_stat: float32 [192, 512, 512], P('fsdp', 'rep'), may hold values from -0.5 to 2, as said below
- right_stat: float32 [192, 512, 512], P('fsdp', 'rep'), may hold values from -0.5 to 2, as said below
- left_root: float32 [192, 512, 512], P('fsdp', 'rep'), may hold values from -0.5 to 1.6, as said below
- right_root: float32 [192, 512, 512], P('fsdp', 'rep'), may hold values from -0.5 to 1.6, as said below
Outputs:
- preconditioned: float32 [4096, 12288], P('fsdp')
- left_next: float32 [192, 512, 512], P('fsdp', 'rep')
- right_next: float32 [192, 512, 512], P('fsdp', 'rep')
The draws below stay inside these ranges and needn't reach their ends.
Inputs may be any that keep to these rules, and one draw needn't show every extreme that they name: `left_stat`: every block is symmetric. `right_stat`: every block is symmetric. `left_root`: every block is symmetric. `right_root`: every block is symmetric.
All inputs are finite; a program needn't handle non-finite values.
Results may differ from the reference program's by a relative error of at most 0.00007.
Values sent between devices are 32-bit elements; how exact they have to be, the bound alone decides.
No kernel may reach another device: no remote copies, remote signals or barrier semaphores. Data moves between devices by JAX's collectives and lax.ppermute only.
A program may use at most 64 MiB of HBM per device.

```python
import math
import jax
import jax.numpy as jnp
from jax import lax

BLOCK = 512
CBLK = 24
ROWS = 4096
COLS = 12288
ROWBLK = 8
NBLK = 192


def symmetric_draw(key, low_diag, high_diag, spread):
    diag_key, off_key = jax.random.split(key)
    diagonal = jax.random.uniform(diag_key, (NBLK, BLOCK), jnp.float32, low_diag, high_diag)
    raw_draw = jax.random.normal(off_key, (NBLK, BLOCK, BLOCK), jnp.float32)
    symmetric = (raw_draw + jnp.swapaxes(raw_draw, 1, 2)) * (spread / math.sqrt(2.0 * BLOCK))
    identity = jnp.eye(BLOCK, dtype=jnp.float32)
    return symmetric * (1.0 - identity) + diagonal[:, :, None] * identity


def draw_left_stat(key, part):
    key = jax.random.fold_in(key, 11)
    return symmetric_draw(key, 0.8, 2.0, 0.25)


def draw_right_stat(key, part):
    key = jax.random.fold_in(key, 12)
    return symmetric_draw(key, 0.8, 2.0, 0.25)


def draw_left_root(key, part):
    key = jax.random.fold_in(key, 13)
    return symmetric_draw(key, 0.6, 1.6, 0.3)


def draw_right_root(key, part):
    key = jax.random.fold_in(key, 14)
    return symmetric_draw(key, 0.6, 1.6, 0.3)


def levels(stream_key, shape, pieces, low, largest):
    def one(dim, parts):
        steps = jax.random.uniform(jax.random.fold_in(jax.random.fold_in(stream_key, 6), dim), (parts,), jnp.float32, low / len(pieces), largest / len(pieces))
        return jnp.repeat(jnp.exp(steps), shape[dim] // parts).reshape((-1,) + (1,) * (len(shape) - dim - 1))

    factor_of = one(*pieces[0])
    for cut in pieces[1:]:
        factor_of = factor_of * one(*cut)
    return factor_of


def centred(own_key, shape, width, bound, cuts=(), kind=jnp.bfloat16):
    entries = jax.random.normal(own_key, shape, jnp.float32) * width
    if len(cuts) > 0:
        entries = levels(own_key, shape, cuts, -0.22, 0.18) * entries
    return jnp.clip(entries, min=-bound, max=bound).astype(kind)


def setup_inputs(seed: int = 0) -> dict:
    key_list = jax.random.split(jax.random.key(seed), 6)
    return {
        "grad": centred(key_list[0], (ROWS, COLS), 1.0, 6.0, ((0, 64),), jnp.float32),
        "left_stat": draw_left_stat(jax.random.fold_in(key_list[5], 71), 0),
        "right_stat": draw_right_stat(jax.random.fold_in(key_list[5], 71), 0),
        "left_root": draw_left_root(jax.random.fold_in(key_list[5], 71), 0),
        "right_root": draw_right_root(jax.random.fold_in(key_list[5], 71), 0),
    }


STAT_DECAY = 0.9


def reference(grad, left_stat, right_stat, left_root, right_root):
    blocks = grad.reshape(ROWBLK, BLOCK, CBLK, BLOCK).transpose(0, 2, 1, 3).reshape(NBLK, BLOCK, BLOCK)

    def update(operands):
        grad_block, left_old, right_old, left_inv, right_inv = operands
        left_gram = jnp.dot(grad_block, grad_block.T, precision=lax.Precision.HIGHEST)
        right_gram = jnp.dot(grad_block.T, grad_block, precision=lax.Precision.HIGHEST)
        left_new = STAT_DECAY * left_old + (1.0 - STAT_DECAY) / BLOCK * left_gram
        right_new = STAT_DECAY * right_old + (1.0 - STAT_DECAY) / BLOCK * right_gram
        applied = jnp.dot(left_inv, grad_block, precision=lax.Precision.HIGHEST)
        precond = jnp.dot(applied, right_inv, precision=lax.Precision.HIGHEST)
        return precond, left_new, right_new

    precond, left_next, right_next = lax.map(update, (blocks, left_stat, right_stat, left_root, right_root))
    preconditioned = precond.reshape(ROWBLK, CBLK, BLOCK, BLOCK).transpose(0, 2, 1, 3).reshape(ROWS, COLS)
    return preconditioned, left_next, right_next
```

```python
import jax
import jax.numpy as jnp
from jax import lax
from jax.experimental import pallas as pl
from jax.experimental.pallas import tpu as pltpu
from jax.sharding import PartitionSpec as P

STAT_DECAY = 0.9
F32 = jnp.float32
BAND = 128
REPLICAS = 4
VMEM_LIMIT = 48 * 1024 * 1024
CHUNKS = ((0,), (1,), (2,))


def split(x):
    high = x.astype(jnp.bfloat16)
    return high, (x - high.astype(F32)).astype(jnp.bfloat16)


def dot3(a, b, dims):
    def one(x, y):
        return lax.dot_general(x, y, (dims, ((), ())), preferred_element_type=F32)

    return one(a[0], b[0]) + (one(a[0], b[1]) + one(a[1], b[0]))


def at(index):
    return pl.ds(pl.multiple_of(index * BAND, BAND), BAND)


def pack_kernel(root_ref, down_ref, up_ref, across_ref):
    me = lax.axis_index("rep")
    after, facing, before = lax.rem(me + 1, 4), lax.rem(me + 2, 4), lax.rem(me + 3, 4)
    for slot in range(3):
        own = root_ref[slot, :, at(me)]
        down_ref[slot] = own
        up_ref[slot] = own
        across_ref[slot] = own
        down_ref[3 + slot] = root_ref[slot, :, at(after)]
        up_ref[3 + slot] = root_ref[slot, :, at(before)]
    down_ref[6] = root_ref[0, :, at(facing)]
    down_ref[7] = root_ref[2, :, at(facing)]
    up_ref[6] = root_ref[1, :, at(facing)]


def pack_roots(left_root):
    tile = lambda n: jax.ShapeDtypeStruct((n, BAND, BAND), F32)
    return pl.pallas_call(pack_kernel, out_shape=(tile(8), tile(7), tile(3)))(left_root)


def apply_kernel(slots, grad_ref, left_ref, above_ref, below_ref, across_ref, right_ref, out_ref, whole):
    me = lax.axis_index("rep")
    after, facing, before = lax.rem(me + 1, 4), lax.rem(me + 2, 4), lax.rem(me + 3, 4)
    for place, slot in enumerate(slots):
        def put(a, b, block):
            whole[at(a), at(b)] = block
            whole[at(b), at(a)] = block.T

        whole[at(me), :] = left_ref[slot]
        for other in (after, facing, before):
            whole[at(other), at(me)] = left_ref[slot, :, at(other)].T
        whole[at(after), at(after)] = above_ref[slot]
        whole[at(before), at(before)] = below_ref[slot]
        whole[at(facing), at(facing)] = across_ref[slot]
        put(after, facing, above_ref[3 + slot])
        put(before, facing, below_ref[3 + slot])
        if slot == 1:
            put(before, after, below_ref[6])
        else:
            put(after, before, above_ref[6 if slot == 0 else 7])
        grad = split(grad_ref[:, slot * 512 : slot * 512 + 512])
        half = dot3(grad, split(right_ref[slot]), ((1,), (1,)))
        out_ref[:, place * BAND : place * BAND + BAND] = dot3(split(whole[...]), split(half), ((1,), (0,)))


def apply_roots(slots, blocks, left_root, above, below, across, right_root):
    def kernel(*refs):
        apply_kernel(slots, *refs)

    return pl.pallas_call(
        kernel,
        out_shape=jax.ShapeDtypeStruct((512, BAND * len(slots)), F32),
        scratch_shapes=[pltpu.VMEM((512, 512), F32)],
        compiler_params=pltpu.CompilerParams(vmem_limit_bytes=VMEM_LIMIT),
        cost_estimate=pl.CostEstimate(
            flops=12 * len(slots) * 512 * 512 * BAND, bytes_accessed=6 << 20, transcendentals=0
        ),
    )(blocks, left_root, above, below, across, right_root)


def gram_kernel(grad_ref, left_ref, right_ref, left_out, right_out):
    me = lax.axis_index("rep")
    grad = split(grad_ref[...])
    rows = split(grad_ref[at(me), :])
    columns = split(grad_ref[:, at(me)].T)
    weight = (1.0 - STAT_DECAY) / 512
    left_out[0] = STAT_DECAY * left_ref[0] + weight * dot3(rows, grad, ((1,), (1,)))
    right_out[0] = STAT_DECAY * right_ref[0] + weight * dot3(columns, grad, ((1,), (0,)))


def grams(blocks, left_stat, right_stat):
    band = pl.BlockSpec((1, BAND, 512), lambda t: (t, 0, 0))
    return pl.pallas_call(
        gram_kernel,
        grid=(3,),
        in_specs=[pl.BlockSpec((512, 512), lambda t: (0, t)), band, band],
        out_specs=[band, band],
        out_shape=(jax.ShapeDtypeStruct((3, BAND, 512), F32),) * 2,
        compiler_params=pltpu.CompilerParams(vmem_limit_bytes=VMEM_LIMIT),
        cost_estimate=pl.CostEstimate(flops=36 * 512 * 512 * BAND, bytes_accessed=7 << 20, transcendentals=0),
    )(blocks, left_stat, right_stat)


def join_kernel(slots, own_ref, before_ref, after_ref, facing_ref, *rest):
    out_ref = rest[-1]
    me = lax.axis_index("rep")
    for shift, ref in ((0, own_ref), (3, before_ref), (1, after_ref), (2, facing_ref)):
        out_ref[:, at(lax.rem(me + shift, 4))] = ref[0]


def join(slot, place, width, pieces, out):
    def kernel(*refs):
        join_kernel((slot,), *refs)

    specs = [pl.BlockSpec((1, 64, BAND), lambda f: (f, 0, place))] * 4
    operands = list(pieces)
    aliases = {}
    if out is not None:
        specs.append(pl.BlockSpec(memory_space=pl.ANY))
        operands.append(out)
        aliases = {4: 0}
    return pl.pallas_call(
        kernel,
        grid=(8,),
        in_specs=specs,
        out_specs=pl.BlockSpec((64, 512), lambda f: (0, 3 * f + slot)),
        out_shape=jax.ShapeDtypeStruct((64, 12288), F32),
        input_output_aliases=aliases,
        compiler_params=pltpu.CompilerParams(vmem_limit_bytes=VMEM_LIMIT),
        cost_estimate=pl.CostEstimate(flops=0, bytes_accessed=2 << 20, transcendentals=0),
    )(*operands)


def shards(grad, left_stat, right_stat, left_root, right_root):
    groups = [[8 * g + p for p in range(8)] for g in range(8)]

    def exchange(x):
        return lax.all_to_all(x, "fsdp", 0, 0, axis_index_groups=groups, tiled=True)

    def shift(x, distance):
        return lax.ppermute(x, "rep", [(i, (i + distance) % REPLICAS) for i in range(REPLICAS)])

    blocks = exchange(jnp.transpose(grad.reshape(64, 8, 1536), (1, 0, 2))).reshape(512, 1536)
    down, up, across = pack_roots(left_root)
    above, below, across = shift(down, 3), shift(up, 1), shift(across, 2)
    out = None
    for slots in CHUNKS:
        width = BAND * len(slots)
        part = apply_roots(slots, blocks, left_root, above, below, across, right_root)
        own = exchange(part.reshape(8, 64, width))
        pieces = (own, shift(own, 1), shift(own, 3), shift(own, 2))
        for place, slot in enumerate(slots):
            out = join(slot, place, width, pieces, out)
    left_next, right_next = grams(blocks, left_stat, right_stat)
    return out, left_next, right_next


def solution(mesh):
    band = P("fsdp", "rep", None)
    return jax.shard_map(
        shards,
        mesh=mesh,
        in_specs=(P("fsdp", None), band, band, band, band),
        out_specs=(P("fsdp", None), band, band),
        check_vma=False,
    )
```

```python
import jax
import jax.numpy as jnp
from jax import lax
from jax.experimental import pallas as pl
from jax.experimental.pallas import tpu as pltpu
from jax.sharding import PartitionSpec as P

STAT_DECAY = 0.9
F32 = jnp.float32
BF16 = jnp.bfloat16
BAND = 128
BLOCK = 512
SLOTS = 3
OWNED = SLOTS * BLOCK
REPLICAS = 4
BANDED = (0, 1)
FILLED = 2
SHIFTS = (1, 3, 2)
HBM = pl.BlockSpec(memory_space=pltpu.HBM)
PARAMS = pltpu.CompilerParams(vmem_limit_bytes=63 * 1024 * 1024 + 512 * 1024)


def array(*shape, dtype=F32):
    return jax.ShapeDtypeStruct(shape, dtype)


def cost(flops, data):
    return pl.CostEstimate(flops=1, bytes_accessed=1, transcendentals=0)


def at(index, size=BAND):
    return pl.ds(pl.multiple_of(index * size, size), size)


def split(x):
    high = x.astype(BF16)
    return high, (x - high.astype(F32)).astype(BF16)


def stacked(x):
    return jnp.concatenate(split(x), axis=0)


def dot_stacked(a, b, dims):
    rows = a.shape[0] // 2

    def one(x, y):
        return lax.dot_general(x, y, (dims, ((), ())), preferred_element_type=F32)

    both = one(a, b[0])
    return both[:rows] + (both[rows:] + one(a[:rows], b[1]))


def dot3(a, b, dims):
    def one(x, y):
        return lax.dot_general(x, y, (dims, ((), ())), preferred_element_type=F32)

    return one(a[0], b[0]) + (one(a[0], b[1]) + one(a[1], b[0]))


def place():
    position = lax.axis_index("fsdp")
    return lax.rem(lax.div(position, 2), 4), lax.rem(position, 2), lax.axis_index("rep")


def run_copies(pairs, sems):
    copies = [pltpu.make_async_copy(src, dst, sems.at[i]) for i, (src, dst) in enumerate(pairs)]
    for copy in copies:
        copy.start()
    for copy in copies:
        copy.wait()


def relay(hops, sems):
    n = len(hops)
    first = [pltpu.make_async_copy(src, mid, sems.at[i]) for i, (src, mid, _) in enumerate(hops)]
    second = [pltpu.make_async_copy(mid, dst, sems.at[n + i]) for i, (_, mid, dst) in enumerate(hops)]
    for copy in first:
        copy.start()
    for arrival, copy in zip(first, second):
        arrival.wait()
        copy.start()
    for copy in second:
        copy.wait()


def dma(n):
    return pltpu.SemaphoreType.DMA((n,))


def copies_of(pairs, sems):
    return [pltpu.make_async_copy(src, dst, sems.at[i]) for i, (src, dst) in enumerate(pairs)]


def deal(grad):
    width = len(BANDED) * BLOCK

    def kernel(grad, out, stage, sems):
        hops = []
        for owner in range(8):
            columns = pl.ds(owner * OWNED, width)
            hops.append((grad.at[:, columns], stage.at[owner], out.at[owner]))
        relay(hops, sems)

    return pl.pallas_call(
        kernel,
        name="deal",
        in_specs=[HBM],
        out_specs=HBM,
        out_shape=array(8, 64, width),
        scratch_shapes=[pltpu.VMEM((8, 64, width), F32), dma(16)],
        compiler_params=PARAMS,
        cost_estimate=cost(0, 4 << 20),
    )(grad)


def deal_core(grad):
    def kernel(grad, out, stage, sems):
        _, core, _ = place()
        hops = []
        for y in range(4):
            start = pl.multiple_of((2 * y + 1 - core) * OWNED + FILLED * BLOCK, BLOCK)
            hops.append((grad.at[:, pl.ds(start, BLOCK)], stage.at[y], out.at[y]))
        relay(hops, sems)

    return pl.pallas_call(
        kernel,
        name="deal_core",
        in_specs=[HBM],
        out_specs=HBM,
        out_shape=array(4, 64, BLOCK),
        scratch_shapes=[pltpu.VMEM((4, 64, BLOCK), F32), dma(8)],
        compiler_params=PARAMS,
        cost_estimate=cost(0, 1 << 20),
    )(grad)


def pack(grad, got):
    def kernel(grad, got, own, *rest):
        *outs, stage, sems = rest
        y, core, _ = place()
        hops = []
        for i, (shift, out) in enumerate(zip((0,) + SHIFTS, (own, *outs))):
            target = lax.rem(y + shift, 4)
            start = pl.multiple_of((2 * target + core) * OWNED + FILLED * BLOCK, BLOCK)
            hops.append((grad.at[:, pl.ds(start, BLOCK)], stage.at[2 * i], out.at[core]))
            hops.append((got.at[target], stage.at[2 * i + 1], out.at[1 - core]))
        relay(hops, sems)

    return pl.pallas_call(
        kernel,
        name="pack",
        in_specs=[HBM] * 2,
        out_specs=[HBM] * 4,
        out_shape=[array(2, 64, BLOCK)] * 4,
        scratch_shapes=[pltpu.VMEM((8, 64, BLOCK), F32), dma(16)],
        compiler_params=PARAMS,
        cost_estimate=cost(0, 2 << 20),
    )(grad, got)


def replicas():
    me = lax.axis_index("rep")
    return [lax.rem(me + i, 4) for i in range(4)]


def pack_roots(roots, picks, diagonals, after_this=None):
    waits = [] if after_this is None else [after_this]
    across_shape = [array(len(diagonals), BAND, BAND)] if diagonals else []

    def kernel(*refs):
        *outs, stage, extra, sems = refs[len(roots) + len(waits) :]
        me, after, facing, before = replicas()
        loads = [(refs[a].at[slot], stage.at[i]) for i, (a, slot) in enumerate(picks)]
        loads += [(refs[a].at[slot, :, at(me)], extra.at[i]) for i, (a, slot) in enumerate(diagonals)]
        run_copies(loads, sems)
        down, up = outs[:2]
        pairs = []
        for i in range(2):
            own = stage.at[i, :, at(me)]
            pairs += [(own, down.at[i]), (own, up.at[i])]
            pairs.append((stage.at[i, :, at(after)], down.at[2 + i]))
            pairs.append((stage.at[i, :, at(before)], up.at[2 + i]))
            pairs.append((stage.at[i, :, at(facing)], (down, up)[i].at[4]))
        if diagonals:
            pairs.append((extra, outs[2]))
        run_copies(pairs, sems)

    return pl.pallas_call(
        kernel,
        name="pack_roots",
        in_specs=[HBM] * (len(roots) + len(waits)),
        out_specs=[HBM] * (2 + len(across_shape)),
        out_shape=[array(5, BAND, BAND)] * 2 + across_shape,
        scratch_shapes=[pltpu.VMEM((2, BAND, BLOCK), F32), pltpu.VMEM((4, BAND, BAND), F32), dma(12)],
        compiler_params=PARAMS,
        cost_estimate=cost(0, 1 << 20),
    )(*roots, *waits)


def whole_roots(roots, picks, above, below, across, first, weight):
    def kernel(*refs):
        *roots, above_in, below_in, across_in, high, low, bands, above, below, across, whole, parts, sems = refs
        me, after, facing, before = replicas()
        pairs = [(roots[a].at[slot], bands.at[i]) for i, (a, slot) in enumerate(picks)]
        run_copies(pairs + [(above_in, above), (below_in, below), (across_in.at[pl.ds(first, 2)], across)], sems)
        stores = []

        def put(a, b, block):
            whole[at(a), at(b)] = block
            whole[at(b), at(a)] = block.T

        for i in range(2):
            whole[at(me), :] = bands[i]
            for other in (after, facing, before):
                whole[at(other), at(me)] = bands[i, :, at(other)].T
            whole[at(after), at(after)] = above[i]
            whole[at(before), at(before)] = below[i]
            whole[at(facing), at(facing)] = across[i]
            put(after, facing, above[2 + i])
            put(before, facing, below[2 + i])
            if i:
                put(before, after, below[4])
            else:
                put(after, before, above[4])
            parts[0, i], parts[1, i] = split(whole[...])
            for j, out in enumerate((high, low)):
                stores.append(pltpu.make_async_copy(parts.at[j, i], out.at[i], sems.at[5 + 2 * i + j]))
                stores[-1].start()
        for copy in stores:
            copy.wait()

    return pl.pallas_call(
        kernel,
        name="whole_roots",
        in_specs=[HBM] * (len(roots) + 3),
        out_specs=[HBM] * 2,
        out_shape=[array(2, BLOCK, BLOCK, dtype=BF16)] * 2,
        scratch_shapes=[
            pltpu.VMEM((2, BAND, BLOCK), F32),
            pltpu.VMEM((5, BAND, BAND), F32),
            pltpu.VMEM((5, BAND, BAND), F32),
            pltpu.VMEM((2, BAND, BAND), F32),
            pltpu.VMEM((BLOCK, BLOCK), F32),
            pltpu.VMEM((2, 2, BLOCK, BLOCK), BF16),
            dma(9),
        ],
        compiler_params=PARAMS,
        cost_estimate=pl.CostEstimate(flops=weight, bytes_accessed=4 << 20, transcendentals=0),
    )(*roots, above, below, across)


def apply_band(blocks, high, low, right_root):
    n = len(BANDED)

    def kernel(blocks, high, low, right, out, grad, parts, right_v, result, sems):
        loads = []
        for i, slot in enumerate(BANDED):
            pairs = [(blocks.at[:, pl.ds(i * BLOCK, BLOCK)], grad.at[i]), (right.at[slot], right_v.at[i])]
            pairs += [(high.at[i], parts.at[i, 0]), (low.at[i], parts.at[i, 1])]
            loads.append([pltpu.make_async_copy(a, b, sems.at[i, j]) for j, (a, b) in enumerate(pairs)])
            for copy in loads[-1]:
                copy.start()
        stores = []
        for i in range(n):
            for copy in loads[i]:
                copy.wait()
            half = dot_stacked(stacked(right_v[i]), split(grad[i]), ((1,), (1,)))
            columns = pl.ds(i * BAND, BAND)
            result[:, columns] = dot_stacked(stacked(half), (parts[i, 0], parts[i, 1]), ((1,), (0,))).T
            stores.append(pltpu.make_async_copy(result.at[:, columns], out.at[:, columns], sems.at[i, 4]))
            stores[-1].start()
        for copy in stores:
            copy.wait()

    return pl.pallas_call(
        kernel,
        name="apply_band",
        in_specs=[HBM] * 4,
        out_specs=HBM,
        out_shape=array(BLOCK, n * BAND),
        scratch_shapes=[
            pltpu.VMEM((n, BLOCK, BLOCK), F32),
            pltpu.VMEM((n, 2, BLOCK, BLOCK), BF16),
            pltpu.VMEM((n, BAND, BLOCK), F32),
            pltpu.VMEM((BLOCK, n * BAND), F32),
            pltpu.SemaphoreType.DMA((n, 5)),
        ],
        compiler_params=PARAMS,
        cost_estimate=cost(n * 12 * BLOCK * BLOCK * BAND, n * 3 << 20),
    )(blocks, high, low, right_root)


def row_pairs(pieces, grad):
    y, _, _ = place()
    pairs = []
    for shift, piece in zip((0,) + SHIFTS, pieces):
        source = lax.rem(y + 4 - shift, 4)
        for core in range(2):
            rows = pl.ds(pl.multiple_of(source * BAND + core * 64, 64), 64)
            pairs.append((piece.at[core], grad.at[rows, :]))
    return pairs


def apply_whole(pieces, high, low):
    def kernel(*refs):
        *pieces, high, low, out, grad, parts, result, sems = refs
        pairs = row_pairs(pieces, grad) + [(high, parts.at[0]), (low, parts.at[1])]
        run_copies(pairs, sems)
        half = dot3(split(grad[...]), (parts[0, 1], parts[1, 1]), ((1,), (0,)))
        result[...] = dot3((parts[0, 0], parts[1, 0]), split(half), ((1,), (0,)))
        run_copies([(result, out)], sems)

    return pl.pallas_call(
        kernel,
        name="apply_whole",
        in_specs=[HBM] * 6,
        out_specs=HBM,
        out_shape=array(BLOCK, BLOCK),
        scratch_shapes=[
            pltpu.VMEM((BLOCK, BLOCK), F32),
            pltpu.VMEM((2, 2, BLOCK, BLOCK), BF16),
            pltpu.VMEM((BLOCK, BLOCK), F32),
            dma(10),
        ],
        compiler_params=PARAMS,
        cost_estimate=cost(12 * BLOCK * BLOCK * BLOCK, 4 << 20),
    )(*pieces, high, low)


def grams(blocks, pieces, left_stat, right_stat):
    def kernel(blocks, *refs):
        *pieces, left, right, left_out, right_out, grad, stats, sems = refs
        me = lax.axis_index("rep")
        loads = []
        for slot in range(SLOTS):
            pairs = [(left.at[slot], stats.at[0, slot]), (right.at[slot], stats.at[1, slot])]
            if slot in BANDED:
                columns = pl.ds(BANDED.index(slot) * BLOCK, BLOCK)
                pairs.append((blocks.at[:, columns], grad.at[slot]))
            else:
                pairs += row_pairs(pieces, grad.at[slot])
            loads.append([pltpu.make_async_copy(a, b, sems.at[slot, i]) for i, (a, b) in enumerate(pairs)])
            for copy in loads[-1]:
                copy.start()
        stores = []
        weight = (1.0 - STAT_DECAY) / BLOCK
        for slot in range(SLOTS):
            for copy in loads[slot]:
                copy.wait()
            whole = split(grad[slot])
            rows = stacked(grad[slot, at(me), :])
            columns = stacked(grad[slot, :, at(me)].T)
            stats[0, slot] = STAT_DECAY * stats[0, slot] + weight * dot_stacked(rows, whole, ((1,), (1,)))
            stats[1, slot] = STAT_DECAY * stats[1, slot] + weight * dot_stacked(columns, whole, ((1,), (0,)))
            for i, out in enumerate((left_out, right_out)):
                stores.append(pltpu.make_async_copy(stats.at[i, slot], out.at[slot], sems.at[slot, 10 + i]))
                stores[-1].start()
        for copy in stores:
            copy.wait()

    return pl.pallas_call(
        kernel,
        name="grams",
        in_specs=[HBM] * 7,
        out_specs=[HBM] * 2,
        out_shape=[array(SLOTS, BAND, BLOCK)] * 2,
        scratch_shapes=[
            pltpu.VMEM((SLOTS, BLOCK, BLOCK), F32),
            pltpu.VMEM((2, SLOTS, BAND, BLOCK), F32),
            pltpu.SemaphoreType.DMA((SLOTS, 12)),
        ],
        compiler_params=PARAMS,
        cost_estimate=pl.CostEstimate(flops=1 << 37, bytes_accessed=7 << 20, transcendentals=0),
    )(blocks, *pieces, left_stat, right_stat)


def join_whole(blocks, out):
    def kernel(blocks, _, out, stage, sems):
        hops = []
        for owner in range(8):
            columns = pl.ds((SLOTS * owner + FILLED) * BLOCK, BLOCK)
            hops.append((blocks.at[owner], stage.at[owner], out.at[:, columns]))
        relay(hops, sems)

    return pl.pallas_call(
        kernel,
        name="join_whole",
        in_specs=[HBM] * 2,
        out_specs=HBM,
        out_shape=array(64, 8 * OWNED),
        scratch_shapes=[pltpu.VMEM((8, 64, BLOCK), F32), dma(16)],
        input_output_aliases={1: 0},
        compiler_params=PARAMS,
        cost_estimate=cost(0, 2 << 20),
    )(blocks, out)


def join_bands(pieces):
    n = len(BANDED)

    def kernel(*refs):
        *pieces, out, bands, rows, sems = refs
        me = replicas()
        loads = []
        for owner in range(8):
            pairs = [(piece.at[owner], bands.at[i, owner]) for i, piece in enumerate(pieces)]
            loads.append([pltpu.make_async_copy(a, b, sems.at[owner, i]) for i, (a, b) in enumerate(pairs)])
            for copy in loads[-1]:
                copy.start()
        stores = []
        for owner in range(8):
            for copy in loads[owner]:
                copy.wait()
            for j, slot in enumerate(BANDED):
                for i, shift in enumerate((0,) + SHIFTS):
                    band = bands[i, owner, :, j * BAND : (j + 1) * BAND]
                    rows[owner, :, at(j * REPLICAS + me[(REPLICAS - shift) % REPLICAS])] = band
                target = out.at[:, pl.ds((SLOTS * owner + slot) * BLOCK, BLOCK)]
                copy = pltpu.make_async_copy(rows.at[owner, :, pl.ds(j * BLOCK, BLOCK)], target, sems.at[owner, 4 + j])
                copy.start()
                stores.append(copy)
        for copy in stores:
            copy.wait()

    return pl.pallas_call(
        kernel,
        name="join_bands",
        in_specs=[HBM] * REPLICAS,
        out_specs=HBM,
        out_shape=array(64, 8 * OWNED),
        scratch_shapes=[
            pltpu.VMEM((REPLICAS, 8, 64, n * BAND), F32),
            pltpu.VMEM((8, 64, n * BLOCK), F32),
            pltpu.SemaphoreType.DMA((8, 4 + n)),
        ],
        compiler_params=PARAMS,
        cost_estimate=cost(0, n * 2 << 20),
    )(*pieces)


def shards(grad, left_stat, right_stat, left_root, right_root):
    groups = [[8 * g + p for p in range(8)] for g in range(8)]
    order = lax.optimization_barrier

    def exchange(x):
        return lax.all_to_all(x, "fsdp", 0, 0, axis_index_groups=groups, tiled=True)

    def along_y(x, distance):
        route = [(i, i - i % 8 + (i % 8 + 2 * distance) % 8) for i in range(64)]
        return lax.ppermute(x, "fsdp", route)

    def along_x(x, distance):
        return lax.ppermute(x, "rep", [(i, (i + distance) % REPLICAS) for i in range(REPLICAS)])

    def other_core(x):
        return lax.ppermute(x, "fsdp", [(i, i ^ 1) for i in range(64)])

    early, late = ((0, 0), (0, 1)), ((0, 2), (1, 2))
    roots = (left_root, right_root)
    dealt, roots = order((deal(grad), roots))
    blocks = exchange(dealt).reshape(BLOCK, len(BANDED) * BLOCK)
    down, up, across = pack_roots(roots, early, early + late)
    across = along_x(across, 2)
    first_whole = whole_roots(roots, early, along_x(down, 3), along_x(up, 1), across, 0, 0)
    down, up = pack_roots(roots, late, (), across)
    second_whole = whole_roots(roots, late, along_x(down, 3), along_x(up, 1), across, 2, 1 << 37)
    got = other_core(deal_core(grad))
    kept, *sent = pack(grad, got)
    pieces = [kept] + [along_y(x, d) for x, d in zip(sent, SHIFTS)]
    own = exchange(apply_band(blocks, *first_whole, right_root).reshape(8, 64, len(BANDED) * BAND))
    own, pieces = order((own, pieces))
    bands = [own] + [along_x(own, d) for d in SHIFTS]
    filled = exchange(apply_whole(pieces, *second_whole).reshape(8, 64, BLOCK))
    out = join_whole(filled, join_bands(bands))
    left_next, right_next = grams(blocks, pieces, left_stat, right_stat)
    return out, left_next, right_next


def solution(mesh):
    band = P("fsdp", "rep", None)
    return jax.shard_map(
        shards,
        mesh=mesh,
        in_specs=(P("fsdp", None), band, band, band, band),
        out_specs=(P("fsdp", None), band, band),
        check_vma=False,
    )
```

```python
import jax
import jax.numpy as jnp
from jax import lax
from jax.experimental import pallas as pl
from jax.experimental.pallas import tpu as pltpu
from jax.sharding import PartitionSpec as P

STAT_DECAY = 0.9
F32 = jnp.float32
BF16 = jnp.bfloat16
BAND = 128
BLOCK = 512
SLOTS = 3
OWNED = SLOTS * BLOCK
REPLICAS = 4
BANDED = (0, 1)
FILLED = 2
SHIFTS = (1, 3, 2)
HBM = pl.BlockSpec(memory_space=pltpu.HBM)
PARAMS = pltpu.CompilerParams(vmem_limit_bytes=63 * 1024 * 1024 + 512 * 1024)


def array(*shape, dtype=F32):
    return jax.ShapeDtypeStruct(shape, dtype)


def cost(flops, data):
    return pl.CostEstimate(flops=1, bytes_accessed=1, transcendentals=0)


def at(index, size=BAND):
    return pl.ds(pl.multiple_of(index * size, size), size)


def split(x):
    high = x.astype(BF16)
    return high, (x - high.astype(F32)).astype(BF16)


def stacked(x):
    return jnp.concatenate(split(x), axis=0)


def dot_stacked(a, b, dims):
    rows = a.shape[0] // 2

    def one(x, y):
        return lax.dot_general(x, y, (dims, ((), ())), preferred_element_type=F32)

    both = one(a, b[0])
    return both[:rows] + (both[rows:] + one(a[:rows], b[1]))


def dot3(a, b, dims):
    def one(x, y):
        return lax.dot_general(x, y, (dims, ((), ())), preferred_element_type=F32)

    return one(a[0], b[0]) + (one(a[0], b[1]) + one(a[1], b[0]))


def place():
    position = lax.axis_index("fsdp")
    return lax.rem(lax.div(position, 2), 4), lax.rem(position, 2), lax.axis_index("rep")


def run_copies(pairs, sems):
    copies = [pltpu.make_async_copy(src, dst, sems.at[i]) for i, (src, dst) in enumerate(pairs)]
    for copy in copies:
        copy.start()
    for copy in copies:
        copy.wait()


def relay(hops, sems):
    n = len(hops)
    first = [pltpu.make_async_copy(src, mid, sems.at[i]) for i, (src, mid, _) in enumerate(hops)]
    second = [pltpu.make_async_copy(mid, dst, sems.at[n + i]) for i, (_, mid, dst) in enumerate(hops)]
    for copy in first:
        copy.start()
    for arrival, copy in zip(first, second):
        arrival.wait()
        copy.start()
    for copy in second:
        copy.wait()


def dma(n):
    return pltpu.SemaphoreType.DMA((n,))


def copies_of(pairs, sems):
    return [pltpu.make_async_copy(src, dst, sems.at[i]) for i, (src, dst) in enumerate(pairs)]


def deal(grad):
    width = len(BANDED) * BLOCK

    def kernel(grad, out, stage, sems):
        hops = []
        for owner in range(8):
            columns = pl.ds(owner * OWNED, width)
            hops.append((grad.at[:, columns], stage.at[owner], out.at[owner]))
        relay(hops, sems)

    return pl.pallas_call(
        kernel,
        name="deal",
        in_specs=[HBM],
        out_specs=HBM,
        out_shape=array(8, 64, width),
        scratch_shapes=[pltpu.VMEM((8, 64, width), F32), dma(16)],
        compiler_params=PARAMS,
        cost_estimate=cost(0, 4 << 20),
    )(grad)


def deal_core(grad):
    def kernel(grad, out, stage, sems):
        _, core, _ = place()
        hops = []
        for y in range(4):
            start = pl.multiple_of((2 * y + 1 - core) * OWNED + FILLED * BLOCK, BLOCK)
            hops.append((grad.at[:, pl.ds(start, BLOCK)], stage.at[y], out.at[y]))
        relay(hops, sems)

    return pl.pallas_call(
        kernel,
        name="deal_core",
        in_specs=[HBM],
        out_specs=HBM,
        out_shape=array(4, 64, BLOCK),
        scratch_shapes=[pltpu.VMEM((4, 64, BLOCK), F32), dma(8)],
        compiler_params=PARAMS,
        cost_estimate=cost(0, 1 << 20),
    )(grad)


def pack(grad, got):
    def kernel(grad, got, own, *rest):
        *outs, stage, sems = rest
        y, core, _ = place()
        hops = []
        for i, (shift, out) in enumerate(zip((0,) + SHIFTS, (own, *outs))):
            target = lax.rem(y + shift, 4)
            start = pl.multiple_of((2 * target + core) * OWNED + FILLED * BLOCK, BLOCK)
            hops.append((grad.at[:, pl.ds(start, BLOCK)], stage.at[2 * i], out.at[core]))
            hops.append((got.at[target], stage.at[2 * i + 1], out.at[1 - core]))
        relay(hops, sems)

    return pl.pallas_call(
        kernel,
        name="pack",
        in_specs=[HBM] * 2,
        out_specs=[HBM] * 4,
        out_shape=[array(2, 64, BLOCK)] * 4,
        scratch_shapes=[pltpu.VMEM((8, 64, BLOCK), F32), dma(16)],
        compiler_params=PARAMS,
        cost_estimate=cost(0, 2 << 20),
    )(grad, got)


def replicas():
    me = lax.axis_index("rep")
    return [lax.rem(me + i, 4) for i in range(4)]


def pack_roots(roots, picks, diagonals, after_this=None):
    waits = [] if after_this is None else [after_this]
    across_shape = [array(len(diagonals), BAND, BAND)] if diagonals else []

    def kernel(*refs):
        *outs, stage, extra, sems = refs[len(roots) + len(waits) :]
        me, after, facing, before = replicas()
        loads = [(refs[a].at[slot], stage.at[i]) for i, (a, slot) in enumerate(picks)]
        loads += [(refs[a].at[slot, :, at(me)], extra.at[i]) for i, (a, slot) in enumerate(diagonals)]
        run_copies(loads, sems)
        down, up = outs[:2]
        pairs = []
        for i in range(2):
            own = stage.at[i, :, at(me)]
            pairs += [(own, down.at[i]), (own, up.at[i])]
            pairs.append((stage.at[i, :, at(after)], down.at[2 + i]))
            pairs.append((stage.at[i, :, at(before)], up.at[2 + i]))
            pairs.append((stage.at[i, :, at(facing)], (down, up)[i].at[4]))
        if diagonals:
            pairs.append((extra, outs[2]))
        run_copies(pairs, sems)

    return pl.pallas_call(
        kernel,
        name="pack_roots",
        in_specs=[HBM] * (len(roots) + len(waits)),
        out_specs=[HBM] * (2 + len(across_shape)),
        out_shape=[array(5, BAND, BAND)] * 2 + across_shape,
        scratch_shapes=[pltpu.VMEM((2, BAND, BLOCK), F32), pltpu.VMEM((4, BAND, BAND), F32), dma(12)],
        compiler_params=PARAMS,
        cost_estimate=cost(0, 1 << 20),
    )(*roots, *waits)


def assemble(i, bands, above, below, across, whole):
    me, after, facing, before = replicas()

    def put(a, b, block):
        whole[at(a), at(b)] = block
        whole[at(b), at(a)] = block.T

    whole[at(me), :] = bands[i]
    for other in (after, facing, before):
        whole[at(other), at(me)] = bands[i, :, at(other)].T
    whole[at(after), at(after)] = above[i]
    whole[at(before), at(before)] = below[i]
    whole[at(facing), at(facing)] = across[i]
    put(after, facing, above[2 + i])
    put(before, facing, below[2 + i])
    if i:
        put(before, after, below[4])
    else:
        put(after, before, above[4])


def root_scratch():
    return [
        pltpu.VMEM((2, BAND, BLOCK), F32),
        pltpu.VMEM((5, BAND, BAND), F32),
        pltpu.VMEM((5, BAND, BAND), F32),
        pltpu.VMEM((2, BAND, BAND), F32),
        pltpu.VMEM((BLOCK, BLOCK), F32),
    ]


def apply_band(blocks, roots, picks, above, below, across, first):
    n = len(BANDED)

    def kernel(*refs):
        blocks, left, right, above_in, below_in, across_in, out = refs[:7]
        bands, above, below, across, whole, grad, right_v, result, sems = refs[7:]
        pairs = [(left.at[slot], bands.at[i]) for i, (_, slot) in enumerate(picks)]
        pairs += [(above_in, above), (below_in, below), (across_in.at[pl.ds(first, 2)], across)]
        pairs += [(right.at[slot], right_v.at[i]) for i, slot in enumerate(BANDED)]
        copies = copies_of(pairs, sems)
        loads = [
            pltpu.make_async_copy(blocks.at[:, pl.ds(i * BLOCK, BLOCK)], grad.at[i], sems.at[len(pairs) + i])
            for i in range(n)
        ]
        for copy in copies + loads:
            copy.start()
        for copy in copies:
            copy.wait()
        stores = []
        for i in range(n):
            assemble(i, bands, above, below, across, whole)
            left_root = split(whole[...])
            loads[i].wait()
            half = dot_stacked(stacked(right_v[i]), split(grad[i]), ((1,), (1,)))
            columns = pl.ds(i * BAND, BAND)
            result[:, columns] = dot_stacked(stacked(half), left_root, ((1,), (0,))).T
            stores.append(pltpu.make_async_copy(result.at[:, columns], out.at[:, columns], sems.at[i]))
            stores[-1].start()
        for copy in stores:
            copy.wait()

    return pl.pallas_call(
        kernel,
        name="apply_band",
        in_specs=[HBM] * 6,
        out_specs=HBM,
        out_shape=array(BLOCK, n * BAND),
        scratch_shapes=root_scratch()
        + [
            pltpu.VMEM((n, BLOCK, BLOCK), F32),
            pltpu.VMEM((n, BAND, BLOCK), F32),
            pltpu.VMEM((BLOCK, n * BAND), F32),
            dma(9),
        ],
        compiler_params=PARAMS,
        cost_estimate=cost(n * 12 * BLOCK * BLOCK * BAND, n * 3 << 20),
    )(blocks, *roots, above, below, across)


def row_pairs(pieces, grad):
    y, _, _ = place()
    pairs = []
    for shift, piece in zip((0,) + SHIFTS, pieces):
        source = lax.rem(y + 4 - shift, 4)
        for core in range(2):
            rows = pl.ds(pl.multiple_of(source * BAND + core * 64, 64), 64)
            pairs.append((piece.at[core], grad.at[rows, :]))
    return pairs


def apply_whole(pieces, roots, picks, above, below, across, first):
    def kernel(*refs):
        pieces, refs = refs[:4], refs[4:]
        *roots, above_in, below_in, across_in, out, bands, above, below, across, whole, grad, result, sems = refs
        pairs = [(roots[a].at[slot], bands.at[i]) for i, (a, slot) in enumerate(picks)]
        pairs += [(above_in, above), (below_in, below), (across_in.at[pl.ds(first, 2)], across)]
        run_copies(pairs + row_pairs(pieces, grad), sems)
        assemble(1, bands, above, below, across, whole)
        half = split(dot3(split(grad[...]), split(whole[...]), ((1,), (0,))))
        assemble(0, bands, above, below, across, whole)
        stores = []
        for i in range(4):
            rows = pl.ds(i * BAND, BAND)
            result[rows, :] = dot_stacked(stacked(whole[rows, :]), half, ((1,), (0,)))
            stores.append(pltpu.make_async_copy(result.at[rows, :], out.at[rows, :], sems.at[i]))
            stores[-1].start()
        for copy in stores:
            copy.wait()

    return pl.pallas_call(
        kernel,
        name="apply_whole",
        in_specs=[HBM] * (7 + len(roots)),
        out_specs=HBM,
        out_shape=array(BLOCK, BLOCK),
        scratch_shapes=root_scratch()
        + [pltpu.VMEM((BLOCK, BLOCK), F32), pltpu.VMEM((BLOCK, BLOCK), F32), dma(13)],
        compiler_params=PARAMS,
        cost_estimate=pl.CostEstimate(flops=1 << 37, bytes_accessed=4 << 20, transcendentals=0),
    )(*pieces, *roots, above, below, across)


def grams(blocks, pieces, left_stat, right_stat):
    def kernel(blocks, *refs):
        *pieces, left, right, left_out, right_out, grad, stats, sems = refs
        me = lax.axis_index("rep")
        loads = []
        for slot in range(SLOTS):
            pairs = [(left.at[slot], stats.at[0, slot]), (right.at[slot], stats.at[1, slot])]
            if slot in BANDED:
                columns = pl.ds(BANDED.index(slot) * BLOCK, BLOCK)
                pairs.append((blocks.at[:, columns], grad.at[slot]))
            else:
                pairs += row_pairs(pieces, grad.at[slot])
            loads.append([pltpu.make_async_copy(a, b, sems.at[slot, i]) for i, (a, b) in enumerate(pairs)])
            for copy in loads[-1]:
                copy.start()
        stores = []
        weight = (1.0 - STAT_DECAY) / BLOCK
        for slot in range(SLOTS):
            for copy in loads[slot]:
                copy.wait()
            whole = split(grad[slot])
            rows = stacked(grad[slot, at(me), :])
            columns = stacked(grad[slot, :, at(me)].T)
            stats[0, slot] = STAT_DECAY * stats[0, slot] + weight * dot_stacked(rows, whole, ((1,), (1,)))
            stats[1, slot] = STAT_DECAY * stats[1, slot] + weight * dot_stacked(columns, whole, ((1,), (0,)))
            for i, out in enumerate((left_out, right_out)):
                stores.append(pltpu.make_async_copy(stats.at[i, slot], out.at[slot], sems.at[slot, 10 + i]))
                stores[-1].start()
        for copy in stores:
            copy.wait()

    return pl.pallas_call(
        kernel,
        name="grams",
        in_specs=[HBM] * 7,
        out_specs=[HBM] * 2,
        out_shape=[array(SLOTS, BAND, BLOCK)] * 2,
        scratch_shapes=[
            pltpu.VMEM((SLOTS, BLOCK, BLOCK), F32),
            pltpu.VMEM((2, SLOTS, BAND, BLOCK), F32),
            pltpu.SemaphoreType.DMA((SLOTS, 12)),
        ],
        compiler_params=PARAMS,
        cost_estimate=pl.CostEstimate(flops=1 << 37, bytes_accessed=7 << 20, transcendentals=0),
    )(blocks, *pieces, left_stat, right_stat)


def join(pieces, filled):
    n = len(BANDED)

    def kernel(*refs):
        *pieces, filled, out, bands, blocks, rows, sems = refs
        me = replicas()
        loads = []
        for owner in range(8):
            pairs = [(piece.at[owner], bands.at[i, owner]) for i, piece in enumerate(pieces)]
            pairs.append((filled.at[owner], blocks.at[owner]))
            loads.append([pltpu.make_async_copy(a, b, sems.at[owner, i]) for i, (a, b) in enumerate(pairs)])
            for copy in loads[-1]:
                copy.start()
        stores = []
        for owner in range(8):
            for copy in loads[owner]:
                copy.wait()
            for j, slot in enumerate(BANDED):
                for i, shift in enumerate((0,) + SHIFTS):
                    band = bands[i, owner, :, j * BAND : (j + 1) * BAND]
                    rows[owner, :, at(j * REPLICAS + me[(REPLICAS - shift) % REPLICAS])] = band
            targets = [(rows.at[owner, :, pl.ds(j * BLOCK, BLOCK)], slot) for j, slot in enumerate(BANDED)]
            for j, (source, slot) in enumerate(targets + [(blocks.at[owner], FILLED)]):
                target = out.at[:, pl.ds((SLOTS * owner + slot) * BLOCK, BLOCK)]
                stores.append(pltpu.make_async_copy(source, target, sems.at[owner, REPLICAS + 1 + j]))
                stores[-1].start()
        for copy in stores:
            copy.wait()

    return pl.pallas_call(
        kernel,
        name="join",
        in_specs=[HBM] * (REPLICAS + 1),
        out_specs=HBM,
        out_shape=array(64, 8 * OWNED),
        scratch_shapes=[
            pltpu.VMEM((REPLICAS, 8, 64, n * BAND), F32),
            pltpu.VMEM((8, 64, BLOCK), F32),
            pltpu.VMEM((8, 64, n * BLOCK), F32),
            pltpu.SemaphoreType.DMA((8, REPLICAS + 1 + SLOTS)),
        ],
        compiler_params=PARAMS,
        cost_estimate=cost(0, 6 << 20),
    )(*pieces, filled)


def shards(grad, left_stat, right_stat, left_root, right_root):
    groups = [[8 * g + p for p in range(8)] for g in range(8)]
    order = lax.optimization_barrier

    def exchange(x):
        return lax.all_to_all(x, "fsdp", 0, 0, axis_index_groups=groups, tiled=True)

    def along_y(x, distance):
        route = [(i, i - i % 8 + (i % 8 + 2 * distance) % 8) for i in range(64)]
        return lax.ppermute(x, "fsdp", route)

    def along_x(x, distance):
        return lax.ppermute(x, "rep", [(i, (i + distance) % REPLICAS) for i in range(REPLICAS)])

    def other_core(x):
        return lax.ppermute(x, "fsdp", [(i, i ^ 1) for i in range(64)])

    early, late = ((0, 0), (0, 1)), ((0, 2), (1, 2))
    roots = (left_root, right_root)
    dealt, roots = order((deal(grad), roots))
    blocks = exchange(dealt).reshape(BLOCK, len(BANDED) * BLOCK)
    down, up, across = pack_roots(roots, early, early + late)
    across = along_x(across, 2)
    second = pack_roots(roots, late, (), across)
    kept, *sent = pack(grad, other_core(deal_core(grad)))
    first = along_x(down, 3), along_x(up, 1)
    second = along_x(second[0], 3), along_x(second[1], 1)
    banded = apply_band(blocks, roots, early, *first, across, 0)
    pieces = [kept] + [along_y(x, d) for x, d in zip(sent, SHIFTS)]
    own = exchange(banded.reshape(8, 64, len(BANDED) * BAND))
    filled = apply_whole(pieces, roots, late, *second, across, 2)
    own, filled = order((own, filled))
    bands = [own] + [along_x(own, d) for d in SHIFTS]
    filled = exchange(filled.reshape(8, 64, BLOCK))
    out = join(bands, filled)
    left_next, right_next = grams(blocks, pieces, left_stat, right_stat)
    return out, left_next, right_next


def solution(mesh):
    band = P("fsdp", "rep", None)
    return jax.shard_map(
        shards,
        mesh=mesh,
        in_specs=(P("fsdp", None), band, band, band, band),
        out_specs=(P("fsdp", None), band, band),
        check_vma=False,
    )
```

```python
import jax
import jax.numpy as jnp
from jax import lax
from jax.experimental import pallas as pl
from jax.experimental.pallas import tpu as pltpu
from jax.sharding import PartitionSpec as P

STAT_DECAY = 0.9
F32 = jnp.float32
BF16 = jnp.bfloat16
BAND = 128
BLOCK = 512
SLOTS = 3
OWNED = SLOTS * BLOCK
REPLICAS = 4
BANDED = (0, 1)
FILLED = 2
SHIFTS = (1, 3, 2)
HBM = pl.BlockSpec(memory_space=pltpu.HBM)
PARAMS = pltpu.CompilerParams(vmem_limit_bytes=63 * 1024 * 1024 + 512 * 1024)


def array(*shape, dtype=F32):
    return jax.ShapeDtypeStruct(shape, dtype)


def cost(flops, data):
    return pl.CostEstimate(flops=1, bytes_accessed=1, transcendentals=0)


def at(index, size=BAND):
    return pl.ds(pl.multiple_of(index * size, size), size)


def split(x):
    high = x.astype(BF16)
    return high, (x - high.astype(F32)).astype(BF16)


def stacked(x):
    return jnp.concatenate(split(x), axis=0)


def dot_stacked(a, b, dims):
    rows = a.shape[0] // 2

    def one(x, y):
        return lax.dot_general(x, y, (dims, ((), ())), preferred_element_type=F32)

    both = one(a, b[0])
    return both[:rows] + (both[rows:] + one(a[:rows], b[1]))


def dot3(a, b, dims):
    def one(x, y):
        return lax.dot_general(x, y, (dims, ((), ())), preferred_element_type=F32)

    return one(a[0], b[0]) + (one(a[0], b[1]) + one(a[1], b[0]))


def place():
    position = lax.axis_index("fsdp")
    return lax.rem(lax.div(position, 2), 4), lax.rem(position, 2), lax.axis_index("rep")


def run_copies(pairs, sems):
    copies = [pltpu.make_async_copy(src, dst, sems.at[i]) for i, (src, dst) in enumerate(pairs)]
    for copy in copies:
        copy.start()
    for copy in copies:
        copy.wait()


def relay(hops, sems):
    n = len(hops)
    first = [pltpu.make_async_copy(src, mid, sems.at[i]) for i, (src, mid, _) in enumerate(hops)]
    second = [pltpu.make_async_copy(mid, dst, sems.at[n + i]) for i, (_, mid, dst) in enumerate(hops)]
    for copy in first:
        copy.start()
    for arrival, copy in zip(first, second):
        arrival.wait()
        copy.start()
    for copy in second:
        copy.wait()


def dma(n):
    return pltpu.SemaphoreType.DMA((n,))


def copies_of(pairs, sems):
    return [pltpu.make_async_copy(src, dst, sems.at[i]) for i, (src, dst) in enumerate(pairs)]


def deal(grad):
    width = len(BANDED) * BLOCK

    def kernel(grad, out, stage, sems):
        hops = []
        for owner in range(8):
            columns = pl.ds(owner * OWNED, width)
            hops.append((grad.at[:, columns], stage.at[owner], out.at[owner]))
        relay(hops, sems)

    return pl.pallas_call(
        kernel,
        name="deal",
        in_specs=[HBM],
        out_specs=HBM,
        out_shape=array(8, 64, width),
        scratch_shapes=[pltpu.VMEM((8, 64, width), F32), dma(16)],
        compiler_params=PARAMS,
        cost_estimate=cost(0, 4 << 20),
    )(grad)


def deal_core(grad):
    def kernel(grad, out, stage, sems):
        _, core, _ = place()
        hops = []
        for y in range(4):
            start = pl.multiple_of((2 * y + 1 - core) * OWNED + FILLED * BLOCK, BLOCK)
            hops.append((grad.at[:, pl.ds(start, BLOCK)], stage.at[y], out.at[y]))
        relay(hops, sems)

    return pl.pallas_call(
        kernel,
        name="deal_core",
        in_specs=[HBM],
        out_specs=HBM,
        out_shape=array(4, 64, BLOCK),
        scratch_shapes=[pltpu.VMEM((4, 64, BLOCK), F32), dma(8)],
        compiler_params=PARAMS,
        cost_estimate=cost(0, 1 << 20),
    )(grad)


def pack(grad, got):
    def kernel(grad, got, own, *rest):
        *outs, stage, sems = rest
        y, core, _ = place()
        hops = []
        for i, (shift, out) in enumerate(zip((0,) + SHIFTS, (own, *outs))):
            target = lax.rem(y + shift, 4)
            start = pl.multiple_of((2 * target + core) * OWNED + FILLED * BLOCK, BLOCK)
            hops.append((grad.at[:, pl.ds(start, BLOCK)], stage.at[2 * i], out.at[core]))
            hops.append((got.at[target], stage.at[2 * i + 1], out.at[1 - core]))
        relay(hops, sems)

    return pl.pallas_call(
        kernel,
        name="pack",
        in_specs=[HBM] * 2,
        out_specs=[HBM] * 4,
        out_shape=[array(2, 64, BLOCK)] * 4,
        scratch_shapes=[pltpu.VMEM((8, 64, BLOCK), F32), dma(16)],
        compiler_params=PARAMS,
        cost_estimate=cost(0, 2 << 20),
    )(grad, got)


def replicas():
    me = lax.axis_index("rep")
    return [lax.rem(me + i, 4) for i in range(4)]


def pack_roots(roots, picks):
    def kernel(*refs):
        *outs, stage, sems = refs[len(roots) :]
        me, after, facing, before = replicas()
        run_copies([(refs[a].at[slot], stage.at[i]) for i, (a, slot) in enumerate(picks)], sems)
        pairs = []
        for i in range(4):
            down, up = outs[1 + i // 2 * 2 : 3 + i // 2 * 2]
            own = stage.at[i, :, at(me)]
            pairs += [(own, outs[0].at[i]), (own, down.at[i % 2]), (own, up.at[i % 2])]
            pairs.append((stage.at[i, :, at(after)], down.at[2 + i % 2]))
            pairs.append((stage.at[i, :, at(before)], up.at[2 + i % 2]))
            pairs.append((stage.at[i, :, at(facing)], (down, up)[i % 2].at[4]))
        run_copies(pairs, sems)

    return pl.pallas_call(
        kernel,
        name="pack_roots",
        in_specs=[HBM] * len(roots),
        out_specs=[HBM] * 5,
        out_shape=[array(4, BAND, BAND)] + [array(5, BAND, BAND)] * 4,
        scratch_shapes=[pltpu.VMEM((4, BAND, BLOCK), F32), dma(24)],
        compiler_params=PARAMS,
        cost_estimate=cost(0, 2 << 20),
    )(*roots)


def follow(x, earlier):
    def kernel(*refs):
        pass

    return pl.pallas_call(
        kernel,
        name="follow",
        in_specs=[HBM] * 2,
        out_specs=HBM,
        out_shape=array(*x.shape),
        input_output_aliases={0: 0},
        compiler_params=PARAMS,
        cost_estimate=cost(0, 0),
    )(x, earlier)


def assemble(i, bands, above, below, across, whole):
    me, after, facing, before = replicas()

    def put(a, b, block):
        whole[at(a), at(b)] = block
        whole[at(b), at(a)] = block.T

    whole[at(me), :] = bands[i]
    for other in (after, facing, before):
        whole[at(other), at(me)] = bands[i, :, at(other)].T
    whole[at(after), at(after)] = above[i]
    whole[at(before), at(before)] = below[i]
    whole[at(facing), at(facing)] = across[i]
    put(after, facing, above[2 + i])
    put(before, facing, below[2 + i])
    if i:
        put(before, after, below[4])
    else:
        put(after, before, above[4])


def root_scratch():
    return [
        pltpu.VMEM((2, BAND, BLOCK), F32),
        pltpu.VMEM((5, BAND, BAND), F32),
        pltpu.VMEM((5, BAND, BAND), F32),
        pltpu.VMEM((2, BAND, BAND), F32),
        pltpu.VMEM((BLOCK, BLOCK), F32),
    ]


def apply_band(blocks, roots, picks, above, below, across, first):
    n = len(BANDED)

    def kernel(*refs):
        blocks, left, right, above_in, below_in, across_in, out = refs[:7]
        bands, above, below, across, whole, grad, right_v, result, sems = refs[7:]
        pairs = [(left.at[slot], bands.at[i]) for i, (_, slot) in enumerate(picks)]
        pairs += [(above_in, above), (below_in, below), (across_in.at[pl.ds(first, 2)], across)]
        pairs += [(right.at[slot], right_v.at[i]) for i, slot in enumerate(BANDED)]
        copies = copies_of(pairs, sems)
        loads = [
            pltpu.make_async_copy(blocks.at[:, pl.ds(i * BLOCK, BLOCK)], grad.at[i], sems.at[len(pairs) + i])
            for i in range(n)
        ]
        for copy in copies + loads:
            copy.start()
        for copy in copies:
            copy.wait()
        stores = []
        for i in range(n):
            assemble(i, bands, above, below, across, whole)
            left_root = split(whole[...])
            loads[i].wait()
            half = dot_stacked(stacked(right_v[i]), split(grad[i]), ((1,), (1,)))
            columns = pl.ds(i * BAND, BAND)
            result[:, columns] = dot_stacked(stacked(half), left_root, ((1,), (0,))).T
            stores.append(pltpu.make_async_copy(result.at[:, columns], out.at[:, columns], sems.at[i]))
            stores[-1].start()
        for copy in stores:
            copy.wait()

    return pl.pallas_call(
        kernel,
        name="apply_band",
        in_specs=[HBM] * 6,
        out_specs=HBM,
        out_shape=array(BLOCK, n * BAND),
        scratch_shapes=root_scratch()
        + [
            pltpu.VMEM((n, BLOCK, BLOCK), F32),
            pltpu.VMEM((n, BAND, BLOCK), F32),
            pltpu.VMEM((BLOCK, n * BAND), F32),
            dma(9),
        ],
        compiler_params=PARAMS,
        cost_estimate=cost(n * 12 * BLOCK * BLOCK * BAND, n * 3 << 20),
    )(blocks, *roots, above, below, across)


def row_pairs(pieces, grad):
    y, _, _ = place()
    pairs = []
    for shift, piece in zip((0,) + SHIFTS, pieces):
        source = lax.rem(y + 4 - shift, 4)
        for core in range(2):
            rows = pl.ds(pl.multiple_of(source * BAND + core * 64, 64), 64)
            pairs.append((piece.at[core], grad.at[rows, :]))
    return pairs


def apply_whole(pieces, roots, picks, above, below, across, first):
    def kernel(*refs):
        pieces, refs = refs[:4], refs[4:]
        *roots, above_in, below_in, across_in, out, bands, above, below, across, whole, grad, result, sems = refs
        pairs = [(roots[a].at[slot], bands.at[i]) for i, (a, slot) in enumerate(picks)]
        pairs += [(above_in, above), (below_in, below), (across_in.at[pl.ds(first, 2)], across)]
        run_copies(pairs + row_pairs(pieces, grad), sems)
        assemble(1, bands, above, below, across, whole)
        half = split(dot3(split(grad[...]), split(whole[...]), ((1,), (0,))))
        assemble(0, bands, above, below, across, whole)
        stores = []
        for i in range(4):
            rows = pl.ds(i * BAND, BAND)
            result[rows, :] = dot_stacked(stacked(whole[rows, :]), half, ((1,), (0,)))
            stores.append(pltpu.make_async_copy(result.at[rows, :], out.at[rows, :], sems.at[i]))
            stores[-1].start()
        for copy in stores:
            copy.wait()

    return pl.pallas_call(
        kernel,
        name="apply_whole",
        in_specs=[HBM] * (7 + len(roots)),
        out_specs=HBM,
        out_shape=array(BLOCK, BLOCK),
        scratch_shapes=root_scratch()
        + [pltpu.VMEM((BLOCK, BLOCK), F32), pltpu.VMEM((BLOCK, BLOCK), F32), dma(13)],
        compiler_params=PARAMS,
        cost_estimate=pl.CostEstimate(flops=1 << 37, bytes_accessed=4 << 20, transcendentals=0),
    )(*pieces, *roots, above, below, across)


def grams(blocks, pieces, left_stat, right_stat):
    def kernel(blocks, *refs):
        *pieces, left, right, left_out, right_out, grad, stats, sems = refs
        me = lax.axis_index("rep")
        loads = []
        for slot in range(SLOTS):
            pairs = [(left.at[slot], stats.at[0, slot]), (right.at[slot], stats.at[1, slot])]
            if slot in BANDED:
                columns = pl.ds(BANDED.index(slot) * BLOCK, BLOCK)
                pairs.append((blocks.at[:, columns], grad.at[slot]))
            else:
                pairs += row_pairs(pieces, grad.at[slot])
            loads.append([pltpu.make_async_copy(a, b, sems.at[slot, i]) for i, (a, b) in enumerate(pairs)])
            for copy in loads[-1]:
                copy.start()
        stores = []
        weight = (1.0 - STAT_DECAY) / BLOCK
        for slot in range(SLOTS):
            for copy in loads[slot]:
                copy.wait()
            whole = split(grad[slot])
            rows = stacked(grad[slot, at(me), :])
            columns = stacked(grad[slot, :, at(me)].T)
            stats[0, slot] = STAT_DECAY * stats[0, slot] + weight * dot_stacked(rows, whole, ((1,), (1,)))
            stats[1, slot] = STAT_DECAY * stats[1, slot] + weight * dot_stacked(columns, whole, ((1,), (0,)))
            for i, out in enumerate((left_out, right_out)):
                stores.append(pltpu.make_async_copy(stats.at[i, slot], out.at[slot], sems.at[slot, 10 + i]))
                stores[-1].start()
        for copy in stores:
            copy.wait()

    return pl.pallas_call(
        kernel,
        name="grams",
        in_specs=[HBM] * 7,
        out_specs=[HBM] * 2,
        out_shape=[array(SLOTS, BAND, BLOCK)] * 2,
        scratch_shapes=[
            pltpu.VMEM((SLOTS, BLOCK, BLOCK), F32),
            pltpu.VMEM((2, SLOTS, BAND, BLOCK), F32),
            pltpu.SemaphoreType.DMA((SLOTS, 12)),
        ],
        compiler_params=PARAMS,
        cost_estimate=cost(36 * BLOCK * BLOCK * BAND, 7 << 20),
    )(blocks, *pieces, left_stat, right_stat)


def join(pieces, filled):
    n = len(BANDED)

    def kernel(*refs):
        *pieces, filled, out, bands, blocks, rows, sems = refs
        _, core, me = place()
        sources = [me, lax.rem(me + 3 - 2 * core, 4), lax.rem(me + 1 + 2 * core, 4), lax.rem(me + 2, 4)]
        loads = []
        for owner in range(8):
            pairs = [(piece.at[owner], bands.at[i, owner]) for i, piece in enumerate(pieces)]
            pairs.append((filled.at[owner], blocks.at[owner]))
            loads.append([pltpu.make_async_copy(a, b, sems.at[owner, i]) for i, (a, b) in enumerate(pairs)])
            for copy in loads[-1]:
                copy.start()
        stores = []
        for owner in range(8):
            for copy in loads[owner]:
                copy.wait()
            for j, slot in enumerate(BANDED):
                for i, source in enumerate(sources):
                    rows[owner, :, at(j * REPLICAS + source)] = bands[i, owner, :, j * BAND : (j + 1) * BAND]
            targets = [(rows.at[owner, :, pl.ds(j * BLOCK, BLOCK)], slot) for j, slot in enumerate(BANDED)]
            for j, (source, slot) in enumerate(targets + [(blocks.at[owner], FILLED)]):
                target = out.at[:, pl.ds((SLOTS * owner + slot) * BLOCK, BLOCK)]
                stores.append(pltpu.make_async_copy(source, target, sems.at[owner, REPLICAS + 1 + j]))
                stores[-1].start()
        for copy in stores:
            copy.wait()

    return pl.pallas_call(
        kernel,
        name="join",
        in_specs=[HBM] * (REPLICAS + 1),
        out_specs=HBM,
        out_shape=array(64, 8 * OWNED),
        scratch_shapes=[
            pltpu.VMEM((REPLICAS, 8, 64, n * BAND), F32),
            pltpu.VMEM((8, 64, BLOCK), F32),
            pltpu.VMEM((8, 64, n * BLOCK), F32),
            pltpu.SemaphoreType.DMA((8, REPLICAS + 1 + SLOTS)),
        ],
        compiler_params=PARAMS,
        cost_estimate=cost(0, 6 << 20),
    )(*pieces, filled)


def shards(grad, left_stat, right_stat, left_root, right_root):
    groups = [[8 * g + p for p in range(8)] for g in range(8)]
    order = lax.optimization_barrier

    def exchange(x):
        return lax.all_to_all(x, "fsdp", 0, 0, axis_index_groups=groups, tiled=True)

    def along_y(x, distance):
        route = [(i, i - i % 8 + (i % 8 + 2 * distance) % 8) for i in range(64)]
        return lax.ppermute(x, "fsdp", route)

    def along_x(x, distance):
        return lax.ppermute(x, "rep", [(i, (i + distance) % REPLICAS) for i in range(REPLICAS)])

    def around(x, direction):
        ends = [(i, r, (r + (1 - 2 * (i % 2)) * direction) % REPLICAS) for i in range(64) for r in range(REPLICAS)]
        return lax.ppermute(x, ("fsdp", "rep"), [(REPLICAS * i + r, REPLICAS * i + t) for i, r, t in ends])

    def other_core(x):
        return lax.ppermute(x, "fsdp", [(i, i ^ 1) for i in range(64)])

    early, late = ((0, 0), (0, 1)), ((0, 2), (1, 2))
    roots = (left_root, right_root)
    dealt, roots = order((deal(grad), roots))
    blocks = exchange(dealt).reshape(BLOCK, len(BANDED) * BLOCK)
    across, *first, down, up = pack_roots(roots, early + late)
    across = along_x(across, 2)
    first = along_x(first[0], 3), along_x(first[1], 1)
    kept, *sent = pack(grad, other_core(deal_core(grad)))
    second = along_x(follow(down, across), 3), along_x(follow(up, across), 1)
    banded = apply_band(blocks, roots, early, *first, across, 0)
    pieces = [kept] + [along_y(x, d) for x, d in zip(sent, SHIFTS)]
    own = exchange(banded.reshape(8, 64, len(BANDED) * BAND))
    filled = apply_whole(pieces, roots, late, *second, across, 2)
    own, filled = order((own, filled))
    near = around(own, 1)
    filled = exchange(filled.reshape(8, 64, BLOCK))
    left_next, right_next = grams(blocks, pieces, left_stat, right_stat)
    out = join([own, near, around(own, -1), around(near, 1)], filled)
    return out, left_next, right_next


def solution(mesh):
    band = P("fsdp", "rep", None)
    return jax.shard_map(
        shards,
        mesh=mesh,
        in_specs=(P("fsdp", None), band, band, band, band),
        out_specs=(P("fsdp", None), band, band),
        check_vma=False,
    )
```

```python
import jax
import jax.numpy as jnp
from jax import lax
from jax.experimental import pallas as pl
from jax.experimental.pallas import tpu as pltpu
from jax.sharding import PartitionSpec as P

STAT_DECAY = 0.9
F32 = jnp.float32
BF16 = jnp.bfloat16
BAND = 128
BLOCK = 512
SLOTS = 3
OWNED = SLOTS * BLOCK
REPLICAS = 4
BANDED = (0, 1)
FILLED = 2
SHIFTS = (1, 3, 2)
HBM = pl.BlockSpec(memory_space=pltpu.HBM)
PARAMS = pltpu.CompilerParams(vmem_limit_bytes=63 * 1024 * 1024 + 512 * 1024)


def array(*shape, dtype=F32):
    return jax.ShapeDtypeStruct(shape, dtype)


def cost(flops, data):
    return pl.CostEstimate(flops=1, bytes_accessed=1, transcendentals=0)


def at(index, size=BAND):
    return pl.ds(pl.multiple_of(index * size, size), size)


def split(x):
    high = x.astype(BF16)
    return high, (x - high.astype(F32)).astype(BF16)


def stacked(x):
    return jnp.concatenate(split(x), axis=0)


def dot_stacked(a, b, dims):
    rows = a.shape[0] // 2

    def one(x, y):
        return lax.dot_general(x, y, (dims, ((), ())), preferred_element_type=F32)

    both = one(a, b[0])
    return both[:rows] + (both[rows:] + one(a[:rows], b[1]))


def dot_beside(a, b):
    columns = b.shape[1] // 2
    both = jnp.dot(a[0], b, preferred_element_type=F32)
    return both[:, :columns] + (both[:, columns:] + jnp.dot(a[1], b[:, :columns], preferred_element_type=F32))


def dot3(a, b, dims):
    def one(x, y):
        return lax.dot_general(x, y, (dims, ((), ())), preferred_element_type=F32)

    return one(a[0], b[0]) + (one(a[0], b[1]) + one(a[1], b[0]))


def place():
    position = lax.axis_index("fsdp")
    return lax.rem(lax.div(position, 2), 4), lax.rem(position, 2), lax.axis_index("rep")


def run_copies(pairs, sems):
    copies = [pltpu.make_async_copy(src, dst, sems.at[i]) for i, (src, dst) in enumerate(pairs)]
    for copy in copies:
        copy.start()
    for copy in copies:
        copy.wait()


def relay(hops, sems):
    n = len(hops)
    first = [pltpu.make_async_copy(src, mid, sems.at[i]) for i, (src, mid, _) in enumerate(hops)]
    second = [pltpu.make_async_copy(mid, dst, sems.at[n + i]) for i, (_, mid, dst) in enumerate(hops)]
    for copy in first:
        copy.start()
    for arrival, copy in zip(first, second):
        arrival.wait()
        copy.start()
    for copy in second:
        copy.wait()


def dma(n):
    return pltpu.SemaphoreType.DMA((n,))


def copies_of(pairs, sems):
    return [pltpu.make_async_copy(src, dst, sems.at[i]) for i, (src, dst) in enumerate(pairs)]


def deal(grad):
    width = len(BANDED) * BLOCK

    def kernel(grad, out, stage, sems):
        hops = []
        for owner in range(8):
            columns = pl.ds(owner * OWNED, width)
            hops.append((grad.at[:, columns], stage.at[owner], out.at[owner]))
        relay(hops, sems)

    return pl.pallas_call(
        kernel,
        name="deal",
        in_specs=[HBM],
        out_specs=HBM,
        out_shape=array(8, 64, width),
        scratch_shapes=[pltpu.VMEM((8, 64, width), F32), dma(16)],
        compiler_params=PARAMS,
        cost_estimate=cost(0, 4 << 20),
    )(grad)


def deal_core(grad):
    def kernel(grad, out, stage, sems):
        _, core, _ = place()
        hops = []
        for y in range(4):
            start = pl.multiple_of((2 * y + 1 - core) * OWNED + FILLED * BLOCK, BLOCK)
            hops.append((grad.at[:, pl.ds(start, BLOCK)], stage.at[y], out.at[y]))
        relay(hops, sems)

    return pl.pallas_call(
        kernel,
        name="deal_core",
        in_specs=[HBM],
        out_specs=HBM,
        out_shape=array(4, 64, BLOCK),
        scratch_shapes=[pltpu.VMEM((4, 64, BLOCK), F32), dma(8)],
        compiler_params=PARAMS,
        cost_estimate=cost(0, 1 << 20),
    )(grad)


def pack(grad, got):
    def kernel(grad, got, own, *rest):
        *outs, stage, sems = rest
        y, core, _ = place()
        hops = []
        for i, (shift, out) in enumerate(zip((0,) + SHIFTS, (own, *outs))):
            target = lax.rem(y + shift, 4)
            start = pl.multiple_of((2 * target + core) * OWNED + FILLED * BLOCK, BLOCK)
            hops.append((grad.at[:, pl.ds(start, BLOCK)], stage.at[2 * i], out.at[core]))
            hops.append((got.at[target], stage.at[2 * i + 1], out.at[1 - core]))
        relay(hops, sems)

    return pl.pallas_call(
        kernel,
        name="pack",
        in_specs=[HBM] * 2,
        out_specs=[HBM] * 4,
        out_shape=[array(2, 64, BLOCK)] * 4,
        scratch_shapes=[pltpu.VMEM((8, 64, BLOCK), F32), dma(16)],
        compiler_params=PARAMS,
        cost_estimate=cost(0, 2 << 20),
    )(grad, got)


def replicas():
    me = lax.axis_index("rep")
    return [lax.rem(me + i, 4) for i in range(4)]


def pack_roots(roots, picks):
    def kernel(*refs):
        *outs, stage, sems = refs[len(roots) :]
        me, after, facing, before = replicas()
        run_copies([(refs[a].at[slot], stage.at[i]) for i, (a, slot) in enumerate(picks)], sems)
        pairs = []
        for i in range(4):
            down, up = outs[1 + i // 2 * 2 : 3 + i // 2 * 2]
            own = stage.at[i, :, at(me)]
            pairs += [(own, outs[0].at[i]), (own, down.at[i % 2]), (own, up.at[i % 2])]
            pairs.append((stage.at[i, :, at(after)], down.at[2 + i % 2]))
            pairs.append((stage.at[i, :, at(before)], up.at[2 + i % 2]))
            pairs.append((stage.at[i, :, at(facing)], (down, up)[i % 2].at[4]))
        run_copies(pairs, sems)

    return pl.pallas_call(
        kernel,
        name="pack_roots",
        in_specs=[HBM] * len(roots),
        out_specs=[HBM] * 5,
        out_shape=[array(4, BAND, BAND)] + [array(5, BAND, BAND)] * 4,
        scratch_shapes=[pltpu.VMEM((4, BAND, BLOCK), F32), dma(24)],
        compiler_params=PARAMS,
        cost_estimate=cost(0, 2 << 20),
    )(*roots)


def follow(x, earlier):
    def kernel(*refs):
        pass

    return pl.pallas_call(
        kernel,
        name="follow",
        in_specs=[HBM] * 2,
        out_specs=HBM,
        out_shape=array(*x.shape),
        input_output_aliases={0: 0},
        compiler_params=PARAMS,
        cost_estimate=cost(0, 0),
    )(x, earlier)


def assemble(i, bands, above, below, across, whole):
    me, after, facing, before = replicas()

    def put(a, b, block):
        whole[at(a), at(b)] = block
        whole[at(b), at(a)] = block.T

    whole[at(me), :] = bands[i]
    for other in (after, facing, before):
        whole[at(other), at(me)] = bands[i, :, at(other)].T
    whole[at(after), at(after)] = above[i]
    whole[at(before), at(before)] = below[i]
    whole[at(facing), at(facing)] = across[i]
    put(after, facing, above[2 + i])
    put(before, facing, below[2 + i])
    if i:
        put(before, after, below[4])
    else:
        put(after, before, above[4])


def root_scratch():
    return [
        pltpu.VMEM((2, BAND, BLOCK), F32),
        pltpu.VMEM((5, BAND, BAND), F32),
        pltpu.VMEM((5, BAND, BAND), F32),
        pltpu.VMEM((2, BAND, BAND), F32),
        pltpu.VMEM((BLOCK, BLOCK), F32),
    ]


def apply_band(blocks, roots, picks, above, below, across, first):
    n = len(BANDED)

    def kernel(*refs):
        blocks, left, right, above_in, below_in, across_in, out = refs[:7]
        bands, above, below, across, whole, grad, right_v, result, sems = refs[7:]
        pairs = [(left.at[slot], bands.at[i]) for i, (_, slot) in enumerate(picks)]
        pairs += [(above_in, above), (below_in, below), (across_in.at[pl.ds(first, 2)], across)]
        pairs += [(right.at[slot], right_v.at[i]) for i, slot in enumerate(BANDED)]
        copies = copies_of(pairs, sems)
        loads = [
            pltpu.make_async_copy(blocks.at[:, pl.ds(i * BLOCK, BLOCK)], grad.at[i], sems.at[len(pairs) + i])
            for i in range(n)
        ]
        for copy in copies + loads:
            copy.start()
        for copy in copies:
            copy.wait()
        stores = []
        for i in range(n):
            assemble(i, bands, above, below, across, whole)
            left_root = split(whole[...])
            loads[i].wait()
            half = dot_beside(split(grad[i]), stacked(right_v[i]).T)
            columns = pl.ds(i * BAND, BAND)
            result[:, columns] = dot_beside(left_root, jnp.concatenate(split(half), axis=1))
            stores.append(pltpu.make_async_copy(result.at[:, columns], out.at[:, columns], sems.at[i]))
            stores[-1].start()
        for copy in stores:
            copy.wait()

    return pl.pallas_call(
        kernel,
        name="apply_band",
        in_specs=[HBM] * 6,
        out_specs=HBM,
        out_shape=array(BLOCK, n * BAND),
        scratch_shapes=root_scratch()
        + [
            pltpu.VMEM((n, BLOCK, BLOCK), F32),
            pltpu.VMEM((n, BAND, BLOCK), F32),
            pltpu.VMEM((BLOCK, n * BAND), F32),
            dma(9),
        ],
        compiler_params=PARAMS,
        cost_estimate=cost(n * 12 * BLOCK * BLOCK * BAND, n * 3 << 20),
    )(blocks, *roots, above, below, across)


def row_pairs(pieces, grad):
    y, _, _ = place()
    pairs = []
    for shift, piece in zip((0,) + SHIFTS, pieces):
        source = lax.rem(y + 4 - shift, 4)
        for core in range(2):
            rows = pl.ds(pl.multiple_of(source * BAND + core * 64, 64), 64)
            pairs.append((piece.at[core], grad.at[rows, :]))
    return pairs


def apply_whole(pieces, roots, picks, above, below, across, first):
    def kernel(*refs):
        pieces, refs = refs[:4], refs[4:]
        *roots, above_in, below_in, across_in, out, bands, above, below, across, whole, grad, result, sems = refs
        pairs = [(roots[a].at[slot], bands.at[i]) for i, (a, slot) in enumerate(picks)]
        pairs += [(above_in, above), (below_in, below), (across_in.at[pl.ds(first, 2)], across)]
        run_copies(pairs + row_pairs(pieces, grad), sems)
        assemble(1, bands, above, below, across, whole)
        half = split(dot3(split(grad[...]), split(whole[...]), ((1,), (0,))))
        assemble(0, bands, above, below, across, whole)
        stores = []
        for i in range(4):
            rows = pl.ds(i * BAND, BAND)
            result[rows, :] = dot_stacked(stacked(whole[rows, :]), half, ((1,), (0,)))
            stores.append(pltpu.make_async_copy(result.at[rows, :], out.at[rows, :], sems.at[i]))
            stores[-1].start()
        for copy in stores:
            copy.wait()

    return pl.pallas_call(
        kernel,
        name="apply_whole",
        in_specs=[HBM] * (7 + len(roots)),
        out_specs=HBM,
        out_shape=array(BLOCK, BLOCK),
        scratch_shapes=root_scratch()
        + [pltpu.VMEM((BLOCK, BLOCK), F32), pltpu.VMEM((BLOCK, BLOCK), F32), dma(13)],
        compiler_params=PARAMS,
        cost_estimate=pl.CostEstimate(flops=1 << 37, bytes_accessed=4 << 20, transcendentals=0),
    )(*pieces, *roots, above, below, across)


def grams(blocks, pieces, left_stat, right_stat):
    def kernel(blocks, *refs):
        *pieces, left, right, left_out, right_out, grad, stats, sems = refs
        me = lax.axis_index("rep")
        loads = []
        for slot in range(SLOTS):
            pairs = [(left.at[slot], stats.at[0, slot]), (right.at[slot], stats.at[1, slot])]
            if slot in BANDED:
                columns = pl.ds(BANDED.index(slot) * BLOCK, BLOCK)
                pairs.append((blocks.at[:, columns], grad.at[slot]))
            else:
                pairs += row_pairs(pieces, grad.at[slot])
            loads.append([pltpu.make_async_copy(a, b, sems.at[slot, i]) for i, (a, b) in enumerate(pairs)])
            for copy in loads[-1]:
                copy.start()
        stores = []
        weight = (1.0 - STAT_DECAY) / BLOCK
        for slot in range(SLOTS):
            for copy in loads[slot]:
                copy.wait()
            whole = split(grad[slot])
            rows = stacked(grad[slot, at(me), :])
            columns = stacked(grad[slot, :, at(me)].T)
            stats[0, slot] = STAT_DECAY * stats[0, slot] + weight * dot_stacked(rows, whole, ((1,), (1,)))
            stats[1, slot] = STAT_DECAY * stats[1, slot] + weight * dot_stacked(columns, whole, ((1,), (0,)))
            for i, out in enumerate((left_out, right_out)):
                stores.append(pltpu.make_async_copy(stats.at[i, slot], out.at[slot], sems.at[slot, 10 + i]))
                stores[-1].start()
        for copy in stores:
            copy.wait()

    return pl.pallas_call(
        kernel,
        name="grams",
        in_specs=[HBM] * 7,
        out_specs=[HBM] * 2,
        out_shape=[array(SLOTS, BAND, BLOCK)] * 2,
        scratch_shapes=[
            pltpu.VMEM((SLOTS, BLOCK, BLOCK), F32),
            pltpu.VMEM((2, SLOTS, BAND, BLOCK), F32),
            pltpu.SemaphoreType.DMA((SLOTS, 12)),
        ],
        compiler_params=PARAMS,
        cost_estimate=cost(36 * BLOCK * BLOCK * BAND, 7 << 20),
    )(blocks, *pieces, left_stat, right_stat)


def join(pieces, filled):
    n = len(BANDED)

    def kernel(*refs):
        *pieces, filled, out, bands, blocks, rows, sems = refs
        _, core, me = place()
        sources = [me, lax.rem(me + 3 - 2 * core, 4), lax.rem(me + 1 + 2 * core, 4), lax.rem(me + 2, 4)]
        loads = []
        for owner in range(8):
            pairs = [(piece.at[owner], bands.at[i, owner]) for i, piece in enumerate(pieces)]
            pairs.append((filled.at[owner], blocks.at[owner]))
            loads.append([pltpu.make_async_copy(a, b, sems.at[owner, i]) for i, (a, b) in enumerate(pairs)])
            for copy in loads[-1]:
                copy.start()
        stores = []
        for owner in range(8):
            for copy in loads[owner]:
                copy.wait()
            for j, slot in enumerate(BANDED):
                for i, source in enumerate(sources):
                    rows[owner, :, at(j * REPLICAS + source)] = bands[i, owner, :, j * BAND : (j + 1) * BAND]
            targets = [(rows.at[owner, :, pl.ds(j * BLOCK, BLOCK)], slot) for j, slot in enumerate(BANDED)]
            for j, (source, slot) in enumerate(targets + [(blocks.at[owner], FILLED)]):
                target = out.at[:, pl.ds((SLOTS * owner + slot) * BLOCK, BLOCK)]
                stores.append(pltpu.make_async_copy(source, target, sems.at[owner, REPLICAS + 1 + j]))
                stores[-1].start()
        for copy in stores:
            copy.wait()

    return pl.pallas_call(
        kernel,
        name="join",
        in_specs=[HBM] * (REPLICAS + 1),
        out_specs=HBM,
        out_shape=array(64, 8 * OWNED),
        scratch_shapes=[
            pltpu.VMEM((REPLICAS, 8, 64, n * BAND), F32),
            pltpu.VMEM((8, 64, BLOCK), F32),
            pltpu.VMEM((8, 64, n * BLOCK), F32),
            pltpu.SemaphoreType.DMA((8, REPLICAS + 1 + SLOTS)),
        ],
        compiler_params=PARAMS,
        cost_estimate=cost(0, 6 << 20),
    )(*pieces, filled)


def shards(grad, left_stat, right_stat, left_root, right_root):
    groups = [[8 * g + p for p in range(8)] for g in range(8)]
    order = lax.optimization_barrier

    def exchange(x):
        return lax.all_to_all(x, "fsdp", 0, 0, axis_index_groups=groups, tiled=True)

    def along_y(x, distance):
        route = [(i, i - i % 8 + (i % 8 + 2 * distance) % 8) for i in range(64)]
        return lax.ppermute(x, "fsdp", route)

    def along_x(x, distance):
        return lax.ppermute(x, "rep", [(i, (i + distance) % REPLICAS) for i in range(REPLICAS)])

    def around(x, direction):
        ends = [(i, r, (r + (1 - 2 * (i % 2)) * direction) % REPLICAS) for i in range(64) for r in range(REPLICAS)]
        return lax.ppermute(x, ("fsdp", "rep"), [(REPLICAS * i + r, REPLICAS * i + t) for i, r, t in ends])

    def other_core(x):
        return lax.ppermute(x, "fsdp", [(i, i ^ 1) for i in range(64)])

    early, late = ((0, 0), (0, 1)), ((0, 2), (1, 2))
    roots = (left_root, right_root)
    dealt, roots = order((deal(grad), roots))
    blocks = exchange(dealt).reshape(BLOCK, len(BANDED) * BLOCK)
    across, *first, down, up = pack_roots(roots, early + late)
    across = along_x(across, 2)
    first = along_x(first[0], 3), along_x(first[1], 1)
    kept, *sent = pack(grad, other_core(deal_core(grad)))
    second = along_x(follow(down, across), 3), along_x(follow(up, across), 1)
    banded = apply_band(blocks, roots, early, *first, across, 0)
    pieces = [kept] + [along_y(x, d) for x, d in zip(sent, SHIFTS)]
    own = exchange(banded.reshape(8, 64, len(BANDED) * BAND))
    filled = apply_whole(pieces, roots, late, *second, across, 2)
    own, filled = order((own, filled))
    near = around(own, 1)
    filled = exchange(filled.reshape(8, 64, BLOCK))
    left_next, right_next = grams(blocks, pieces, left_stat, right_stat)
    out = join([own, near, around(own, -1), around(near, 1)], filled)
    return out, left_next, right_next


def solution(mesh):
    band = P("fsdp", "rep", None)
    return jax.shard_map(
        shards,
        mesh=mesh,
        in_specs=(P("fsdp", None), band, band, band, band),
        out_specs=(P("fsdp", None), band, band),
        check_vma=False,
    )
```

```python
import jax
import jax.numpy as jnp
from jax import lax
from jax.experimental import pallas as pl
from jax.experimental.pallas import tpu as pltpu
from jax.sharding import PartitionSpec as P

STAT_DECAY = 0.9
F32 = jnp.float32
BF16 = jnp.bfloat16
BAND = 128
BLOCK = 512
SLOTS = 3
OWNED = SLOTS * BLOCK
REPLICAS = 4
BANDED = (0, 1)
FILLED = 2
SHIFTS = (1, 3, 2)
HBM = pl.BlockSpec(memory_space=pltpu.HBM)
VMEM = pl.BlockSpec(memory_space=pltpu.VMEM)
PARAMS = pltpu.CompilerParams(vmem_limit_bytes=63 * 1024 * 1024 + 512 * 1024)
SMALL = pltpu.CompilerParams(vmem_limit_bytes=32 * 1024 * 1024)


def array(*shape, dtype=F32):
    return jax.ShapeDtypeStruct(shape, dtype)


def cost(flops, data):
    return pl.CostEstimate(flops=1, bytes_accessed=1, transcendentals=0)


def at(index, size=BAND):
    return pl.ds(pl.multiple_of(index * size, size), size)


def split(x):
    high = x.astype(BF16)
    return high, (x - high.astype(F32)).astype(BF16)


def stacked(x):
    return jnp.concatenate(split(x), axis=0)


def dot_stacked(a, b, dims):
    rows = a.shape[0] // 2

    def one(x, y):
        return lax.dot_general(x, y, (dims, ((), ())), preferred_element_type=F32)

    both = one(a, b[0])
    return both[:rows] + (both[rows:] + one(a[:rows], b[1]))


def dot_beside(a, b):
    columns = b.shape[1] // 2
    both = jnp.dot(a[0], b, preferred_element_type=F32)
    return both[:, :columns] + (both[:, columns:] + jnp.dot(a[1], b[:, :columns], preferred_element_type=F32))


def dot3(a, b, dims):
    def one(x, y):
        return lax.dot_general(x, y, (dims, ((), ())), preferred_element_type=F32)

    return one(a[0], b[0]) + (one(a[0], b[1]) + one(a[1], b[0]))


def place():
    position = lax.axis_index("fsdp")
    return lax.rem(lax.div(position, 2), 4), lax.rem(position, 2), lax.axis_index("rep")


def run_copies(pairs, sems):
    copies = [pltpu.make_async_copy(src, dst, sems.at[i]) for i, (src, dst) in enumerate(pairs)]
    for copy in copies:
        copy.start()
    for copy in copies:
        copy.wait()


def relay(hops, sems):
    n = len(hops)
    first = [pltpu.make_async_copy(src, mid, sems.at[i]) for i, (src, mid, _) in enumerate(hops)]
    second = [pltpu.make_async_copy(mid, dst, sems.at[n + i]) for i, (_, mid, dst) in enumerate(hops)]
    for copy in first:
        copy.start()
    for arrival, copy in zip(first, second):
        arrival.wait()
        copy.start()
    for copy in second:
        copy.wait()


def dma(n):
    return pltpu.SemaphoreType.DMA((n,))


def copies_of(pairs, sems):
    return [pltpu.make_async_copy(src, dst, sems.at[i]) for i, (src, dst) in enumerate(pairs)]


def deal(grad):
    width = len(BANDED) * BLOCK

    def kernel(grad, out, stage, sems):
        hops = []
        for owner in range(8):
            columns = pl.ds(owner * OWNED, width)
            hops.append((grad.at[:, columns], stage.at[owner], out.at[owner]))
        relay(hops, sems)

    return pl.pallas_call(
        kernel,
        name="deal",
        in_specs=[HBM],
        out_specs=HBM,
        out_shape=array(8, 64, width),
        scratch_shapes=[pltpu.VMEM((8, 64, width), F32), dma(16)],
        compiler_params=PARAMS,
        cost_estimate=cost(0, 4 << 20),
    )(grad)


def deal_core(grad):
    def kernel(grad, out, stage, sems):
        _, core, _ = place()
        hops = []
        for y in range(4):
            start = pl.multiple_of((2 * y + 1 - core) * OWNED + FILLED * BLOCK, BLOCK)
            hops.append((grad.at[:, pl.ds(start, BLOCK)], stage.at[y], out.at[y]))
        relay(hops, sems)

    return pl.pallas_call(
        kernel,
        name="deal_core",
        in_specs=[HBM],
        out_specs=HBM,
        out_shape=array(4, 64, BLOCK),
        scratch_shapes=[pltpu.VMEM((4, 64, BLOCK), F32), dma(8)],
        compiler_params=PARAMS,
        cost_estimate=cost(0, 1 << 20),
    )(grad)


def pack(grad, got):
    def kernel(grad, got, own, *rest):
        *outs, stage, sems = rest
        y, core, _ = place()
        hops = []
        for i, (shift, out) in enumerate(zip((0,) + SHIFTS, (own, *outs))):
            target = lax.rem(y + shift, 4)
            start = pl.multiple_of((2 * target + core) * OWNED + FILLED * BLOCK, BLOCK)
            hops.append((grad.at[:, pl.ds(start, BLOCK)], stage.at[2 * i], out.at[core]))
            hops.append((got.at[target], stage.at[2 * i + 1], out.at[1 - core]))
        relay(hops, sems)

    return pl.pallas_call(
        kernel,
        name="pack",
        in_specs=[HBM] * 2,
        out_specs=[HBM] * 4,
        out_shape=[array(2, 64, BLOCK)] * 4,
        scratch_shapes=[pltpu.VMEM((8, 64, BLOCK), F32), dma(16)],
        compiler_params=PARAMS,
        cost_estimate=cost(0, 2 << 20),
    )(grad, got)


def replicas():
    me = lax.axis_index("rep")
    return [lax.rem(me + i, 4) for i in range(4)]


def pack_roots(roots, picks):
    def kernel(*refs):
        *outs, stage, sems = refs[len(roots) :]
        me, after, facing, before = replicas()
        run_copies([(refs[a].at[slot], stage.at[i]) for i, (a, slot) in enumerate(picks)], sems)
        pairs = []
        for i in range(4):
            down, up = outs[1 + i // 2 * 2 : 3 + i // 2 * 2]
            own = stage.at[i, :, at(me)]
            pairs += [(own, outs[0].at[i]), (own, down.at[i % 2]), (own, up.at[i % 2])]
            pairs.append((stage.at[i, :, at(after)], down.at[2 + i % 2]))
            pairs.append((stage.at[i, :, at(before)], up.at[2 + i % 2]))
            pairs.append((stage.at[i, :, at(facing)], (down, up)[i % 2].at[4]))
        run_copies(pairs, sems)

    return pl.pallas_call(
        kernel,
        name="pack_roots",
        in_specs=[HBM] * len(roots),
        out_specs=[HBM] * 5,
        out_shape=[array(4, BAND, BAND)] + [array(5, BAND, BAND)] * 4,
        scratch_shapes=[pltpu.VMEM((4, BAND, BLOCK), F32), dma(24)],
        compiler_params=PARAMS,
        cost_estimate=cost(0, 2 << 20),
    )(*roots)


def follow(x, earlier):
    def kernel(*refs):
        pass

    return pl.pallas_call(
        kernel,
        name="follow",
        in_specs=[HBM] * 2,
        out_specs=HBM,
        out_shape=array(*x.shape),
        input_output_aliases={0: 0},
        compiler_params=PARAMS,
        cost_estimate=cost(0, 0),
    )(x, earlier)


def assemble(i, bands, above, below, across, whole):
    me, after, facing, before = replicas()

    def put(a, b, block):
        whole[at(a), at(b)] = block
        whole[at(b), at(a)] = block.T

    whole[at(me), :] = bands[i]
    for other in (after, facing, before):
        whole[at(other), at(me)] = bands[i, :, at(other)].T
    whole[at(after), at(after)] = above[i]
    whole[at(before), at(before)] = below[i]
    whole[at(facing), at(facing)] = across[i]
    put(after, facing, above[2 + i])
    put(before, facing, below[2 + i])
    if i:
        put(before, after, below[4])
    else:
        put(after, before, above[4])


def root_scratch():
    return [
        pltpu.VMEM((2, BAND, BLOCK), F32),
        pltpu.VMEM((5, BAND, BAND), F32),
        pltpu.VMEM((5, BAND, BAND), F32),
        pltpu.VMEM((2, BAND, BAND), F32),
        pltpu.VMEM((BLOCK, BLOCK), F32),
    ]


def apply_band(blocks, roots, picks, above, below, across, first):
    n = len(BANDED)

    def kernel(*refs):
        blocks, left, right, above_in, below_in, across_in, out = refs[:7]
        bands, above, below, across, whole, grad, right_v, result, sems = refs[7:]
        pairs = [(left.at[slot], bands.at[i]) for i, (_, slot) in enumerate(picks)]
        pairs += [(above_in, above), (below_in, below), (across_in.at[pl.ds(first, 2)], across)]
        pairs += [(right.at[slot], right_v.at[i]) for i, slot in enumerate(BANDED)]
        copies = copies_of(pairs, sems)
        loads = [
            pltpu.make_async_copy(blocks.at[:, pl.ds(i * BLOCK, BLOCK)], grad.at[i], sems.at[len(pairs) + i])
            for i in range(n)
        ]
        for copy in copies + loads:
            copy.start()
        for copy in copies:
            copy.wait()
        stores = []
        for i in range(n):
            assemble(i, bands, above, below, across, whole)
            left_root = split(whole[...])
            loads[i].wait()
            half = dot_beside(split(grad[i]), stacked(right_v[i]).T)
            columns = pl.ds(i * BAND, BAND)
            result[:, columns] = dot_beside(left_root, jnp.concatenate(split(half), axis=1))
            stores.append(pltpu.make_async_copy(result.at[:, columns], out.at[:, columns], sems.at[i]))
            stores[-1].start()
        for copy in stores:
            copy.wait()

    return pl.pallas_call(
        kernel,
        name="apply_band",
        in_specs=[HBM] * 6,
        out_specs=HBM,
        out_shape=array(BLOCK, n * BAND),
        scratch_shapes=root_scratch()
        + [
            pltpu.VMEM((n, BLOCK, BLOCK), F32),
            pltpu.VMEM((n, BAND, BLOCK), F32),
            pltpu.VMEM((BLOCK, n * BAND), F32),
            dma(9),
        ],
        compiler_params=PARAMS,
        cost_estimate=cost(n * 12 * BLOCK * BLOCK * BAND, n * 3 << 20),
    )(blocks, *roots, above, below, across)


def row_pairs(pieces, grad):
    y, _, _ = place()
    pairs = []
    for shift, piece in zip((0,) + SHIFTS, pieces):
        source = lax.rem(y + 4 - shift, 4)
        for core in range(2):
            rows = pl.ds(pl.multiple_of(source * BAND + core * 64, 64), 64)
            pairs.append((piece.at[core], grad.at[rows, :]))
    return pairs


def apply_whole(pieces, roots, picks, above, below, across, first):
    def kernel(*refs):
        pieces, refs = refs[:4], refs[4:]
        *roots, above_in, below_in, across_in, out, bands, above, below, across, whole, grad, result, sems = refs
        pairs = [(roots[a].at[slot], bands.at[i]) for i, (a, slot) in enumerate(picks)]
        pairs += [(above_in, above), (below_in, below), (across_in.at[pl.ds(first, 2)], across)]
        run_copies(pairs + row_pairs(pieces, grad), sems)
        assemble(1, bands, above, below, across, whole)
        half = split(dot3(split(grad[...]), split(whole[...]), ((1,), (0,))))
        assemble(0, bands, above, below, across, whole)
        stores = []
        for i in range(4):
            rows = pl.ds(i * BAND, BAND)
            result[rows, :] = dot_stacked(stacked(whole[rows, :]), half, ((1,), (0,)))
            stores.append(pltpu.make_async_copy(result.at[rows, :], out.at[rows, :], sems.at[i]))
            stores[-1].start()
        for copy in stores:
            copy.wait()

    return pl.pallas_call(
        kernel,
        name="apply_whole",
        in_specs=[HBM] * (7 + len(roots)),
        out_specs=HBM,
        out_shape=array(BLOCK, BLOCK),
        scratch_shapes=root_scratch()
        + [pltpu.VMEM((BLOCK, BLOCK), F32), pltpu.VMEM((BLOCK, BLOCK), F32), dma(13)],
        compiler_params=PARAMS,
        cost_estimate=pl.CostEstimate(flops=1 << 37, bytes_accessed=4 << 20, transcendentals=0),
    )(*pieces, *roots, above, below, across)


def grams(blocks, pieces, left_stat, right_stat):
    def kernel(blocks, *refs):
        *pieces, left, right, left_out, right_out, grad, stats, sems = refs
        me = lax.axis_index("rep")
        loads = []
        for slot in range(SLOTS):
            pairs = [(left.at[slot], stats.at[0, slot]), (right.at[slot], stats.at[1, slot])]
            if slot in BANDED:
                columns = pl.ds(BANDED.index(slot) * BLOCK, BLOCK)
                pairs.append((blocks.at[:, columns], grad.at[slot]))
            else:
                pairs += row_pairs(pieces, grad.at[slot])
            loads.append([pltpu.make_async_copy(a, b, sems.at[slot, i]) for i, (a, b) in enumerate(pairs)])
            for copy in loads[-1]:
                copy.start()
        stores = []
        weight = (1.0 - STAT_DECAY) / BLOCK
        for slot in range(SLOTS):
            for copy in loads[slot]:
                copy.wait()
            whole = split(grad[slot])
            rows = stacked(grad[slot, at(me), :])
            columns = stacked(grad[slot, :, at(me)].T)
            stats[0, slot] = STAT_DECAY * stats[0, slot] + weight * dot_stacked(rows, whole, ((1,), (1,)))
            stats[1, slot] = STAT_DECAY * stats[1, slot] + weight * dot_stacked(columns, whole, ((1,), (0,)))
            for i, out in enumerate((left_out, right_out)):
                stores.append(pltpu.make_async_copy(stats.at[i, slot], out.at[slot], sems.at[slot, 10 + i]))
                stores[-1].start()
        for copy in stores:
            copy.wait()

    return pl.pallas_call(
        kernel,
        name="grams",
        in_specs=[HBM] * 7,
        out_specs=[HBM] * 2,
        out_shape=[array(SLOTS, BAND, BLOCK)] * 2,
        scratch_shapes=[
            pltpu.VMEM((SLOTS, BLOCK, BLOCK), F32),
            pltpu.VMEM((2, SLOTS, BAND, BLOCK), F32),
            pltpu.SemaphoreType.DMA((SLOTS, 12)),
        ],
        compiler_params=SMALL,
        cost_estimate=cost(36 * BLOCK * BLOCK * BAND, 7 << 20),
    )(blocks, *pieces, left_stat, right_stat)


def join(pieces, filled):
    n = len(BANDED)

    def kernel(own, near, other, far, filled, out, own_v, rows, sems):
        _, core, me = place()
        load = pltpu.make_async_copy(own, own_v, sems.at[8, 0])
        load.start()
        stores = []
        for owner in range(8):
            target = out.at[:, pl.ds((SLOTS * owner + FILLED) * BLOCK, BLOCK)]
            stores.append(pltpu.make_async_copy(filled.at[owner], target, sems.at[owner, 0]))
            stores[-1].start()
        sources = (lax.rem(me + 3 - 2 * core, 4), lax.rem(me + 1 + 2 * core, 4), lax.rem(me + 2, 4), me)
        load.wait()
        for owner in range(8):
            for j, slot in enumerate(BANDED):
                for bands, source in zip((near, other, far, own_v), sources):
                    rows[owner, :, at(j * REPLICAS + source)] = bands[owner, :, j * BAND : (j + 1) * BAND]
                target = out.at[:, pl.ds((SLOTS * owner + slot) * BLOCK, BLOCK)]
                copy = pltpu.make_async_copy(rows.at[owner, :, pl.ds(j * BLOCK, BLOCK)], target, sems.at[owner, 1 + j])
                copy.start()
                stores.append(copy)
        for copy in stores:
            copy.wait()

    return pl.pallas_call(
        kernel,
        name="join",
        in_specs=[HBM] + [VMEM] * 4,
        out_specs=HBM,
        out_shape=array(64, 8 * OWNED),
        scratch_shapes=[
            pltpu.VMEM((8, 64, n * BAND), F32),
            pltpu.VMEM((8, 64, n * BLOCK), F32),
            pltpu.SemaphoreType.DMA((9, 1 + n)),
        ],
        compiler_params=SMALL,
        cost_estimate=cost(0, 6 << 20),
    )(*pieces, filled)


def shards(grad, left_stat, right_stat, left_root, right_root):
    groups = [[8 * g + p for p in range(8)] for g in range(8)]
    order = lax.optimization_barrier

    def exchange(x):
        return lax.all_to_all(x, "fsdp", 0, 0, axis_index_groups=groups, tiled=True)

    def along_y(x, distance):
        route = [(i, i - i % 8 + (i % 8 + 2 * distance) % 8) for i in range(64)]
        return lax.ppermute(x, "fsdp", route)

    def along_x(x, distance):
        return lax.ppermute(x, "rep", [(i, (i + distance) % REPLICAS) for i in range(REPLICAS)])

    def around(x, direction):
        ends = [(i, r, (r + (1 - 2 * (i % 2)) * direction) % REPLICAS) for i in range(64) for r in range(REPLICAS)]
        return lax.ppermute(x, ("fsdp", "rep"), [(REPLICAS * i + r, REPLICAS * i + t) for i, r, t in ends])

    def other_core(x):
        return lax.ppermute(x, "fsdp", [(i, i ^ 1) for i in range(64)])

    early, late = ((0, 0), (0, 1)), ((0, 2), (1, 2))
    roots = (left_root, right_root)
    dealt, roots = order((deal(grad), roots))
    blocks = exchange(dealt).reshape(BLOCK, len(BANDED) * BLOCK)
    across, *first, down, up = pack_roots(roots, early + late)
    across = along_x(across, 2)
    first = along_x(first[0], 3), along_x(first[1], 1)
    kept, *sent = pack(grad, other_core(deal_core(grad)))
    second = along_x(follow(down, across), 3), along_x(follow(up, across), 1)
    banded = apply_band(blocks, roots, early, *first, across, 0)
    pieces = [kept] + [along_y(x, d) for x, d in zip(sent, SHIFTS)]
    own = exchange(banded.reshape(8, 64, len(BANDED) * BAND))
    filled = apply_whole(pieces, roots, late, *second, across, 2)
    own, filled = order((own, filled))
    near = around(own, 1)
    filled = exchange(filled.reshape(8, 64, BLOCK))
    left_next, right_next = grams(blocks, pieces, left_stat, right_stat)
    out = join([own, near, around(own, -1), around(near, 1)], filled)
    return out, left_next, right_next


def solution(mesh):
    band = P("fsdp", "rep", None)
    return jax.shard_map(
        shards,
        mesh=mesh,
        in_specs=(P("fsdp", None), band, band, band, band),
        out_specs=(P("fsdp", None), band, band),
        check_vma=False,
    )
```

```python
import jax
import jax.numpy as jnp
from jax import lax
from jax.experimental import pallas as pl
from jax.experimental.pallas import tpu as pltpu
from jax.sharding import PartitionSpec as P

STAT_DECAY = 0.9
F32 = jnp.float32
BF16 = jnp.bfloat16
BAND = 128
BLOCK = 512
SLOTS = 3
OWNED = SLOTS * BLOCK
REPLICAS = 4
BANDED = (0, 1)
FILLED = 2
SHIFTS = (1, 3, 2)
HBM = pl.BlockSpec(memory_space=pltpu.HBM)
VMEM = pl.BlockSpec(memory_space=pltpu.VMEM)
PARAMS = pltpu.CompilerParams(vmem_limit_bytes=63 * 1024 * 1024 + 512 * 1024)
SMALL = pltpu.CompilerParams(vmem_limit_bytes=32 * 1024 * 1024)


def array(*shape, dtype=F32):
    return jax.ShapeDtypeStruct(shape, dtype)


def cost(flops, data):
    return pl.CostEstimate(flops=1, bytes_accessed=1, transcendentals=0)


def at(index, size=BAND):
    return pl.ds(pl.multiple_of(index * size, size), size)


def split(x):
    high = x.astype(BF16)
    return high, (x - high.astype(F32)).astype(BF16)


def stacked(x):
    return jnp.concatenate(split(x), axis=0)


def dot_stacked(a, b, dims):
    rows = a.shape[0] // 2

    def one(x, y):
        return lax.dot_general(x, y, (dims, ((), ())), preferred_element_type=F32)

    both = one(a, b[0])
    return both[:rows] + (both[rows:] + one(a[:rows], b[1]))


def dot_beside(a, b):
    columns = b.shape[1] // 2
    both = jnp.dot(a[0], b, preferred_element_type=F32)
    return both[:, :columns] + (both[:, columns:] + jnp.dot(a[1], b[:, :columns], preferred_element_type=F32))


def dot3(a, b, dims):
    def one(x, y):
        return lax.dot_general(x, y, (dims, ((), ())), preferred_element_type=F32)

    return one(a[0], b[0]) + (one(a[0], b[1]) + one(a[1], b[0]))


def place():
    position = lax.axis_index("fsdp")
    return lax.rem(lax.div(position, 2), 4), lax.rem(position, 2), lax.axis_index("rep")


def run_copies(pairs, sems):
    copies = [pltpu.make_async_copy(src, dst, sems.at[i]) for i, (src, dst) in enumerate(pairs)]
    for copy in copies:
        copy.start()
    for copy in copies:
        copy.wait()


def relay(hops, sems):
    n = len(hops)
    first = [pltpu.make_async_copy(src, mid, sems.at[i]) for i, (src, mid, _) in enumerate(hops)]
    second = [pltpu.make_async_copy(mid, dst, sems.at[n + i]) for i, (_, mid, dst) in enumerate(hops)]
    for copy in first:
        copy.start()
    for arrival, copy in zip(first, second):
        arrival.wait()
        copy.start()
    for copy in second:
        copy.wait()


def dma(n):
    return pltpu.SemaphoreType.DMA((n,))


def copies_of(pairs, sems):
    return [pltpu.make_async_copy(src, dst, sems.at[i]) for i, (src, dst) in enumerate(pairs)]


def deal(grad):
    width = len(BANDED) * BLOCK

    def kernel(grad, out, stage, sems):
        hops = []
        for owner in range(8):
            columns = pl.ds(owner * OWNED, width)
            hops.append((grad.at[:, columns], stage.at[owner], out.at[owner]))
        relay(hops, sems)

    return pl.pallas_call(
        kernel,
        name="deal",
        in_specs=[HBM],
        out_specs=HBM,
        out_shape=array(8, 64, width),
        scratch_shapes=[pltpu.VMEM((8, 64, width), F32), dma(16)],
        compiler_params=PARAMS,
        cost_estimate=cost(0, 4 << 20),
    )(grad)


def deal_core(grad):
    def kernel(grad, out, stage, sems):
        _, core, _ = place()
        hops = []
        for y in range(4):
            start = pl.multiple_of((2 * y + 1 - core) * OWNED + FILLED * BLOCK, BLOCK)
            hops.append((grad.at[:, pl.ds(start, BLOCK)], stage.at[y], out.at[y]))
        relay(hops, sems)

    return pl.pallas_call(
        kernel,
        name="deal_core",
        in_specs=[HBM],
        out_specs=HBM,
        out_shape=array(4, 64, BLOCK),
        scratch_shapes=[pltpu.VMEM((4, 64, BLOCK), F32), dma(8)],
        compiler_params=SMALL,
        cost_estimate=cost(0, 1 << 20),
    )(grad)


def pack(grad, got):
    def kernel(grad, got, own, *rest):
        *outs, stage, sems = rest
        y, core, _ = place()
        hops = []
        for i, (shift, out) in enumerate(zip((0,) + SHIFTS, (own, *outs))):
            target = lax.rem(y + shift, 4)
            start = pl.multiple_of((2 * target + core) * OWNED + FILLED * BLOCK, BLOCK)
            hops.append((grad.at[:, pl.ds(start, BLOCK)], stage.at[2 * i], out.at[core]))
            hops.append((got.at[target], stage.at[2 * i + 1], out.at[1 - core]))
        relay(hops, sems)

    return pl.pallas_call(
        kernel,
        name="pack",
        in_specs=[HBM] * 2,
        out_specs=[HBM] * 4,
        out_shape=[array(2, 64, BLOCK)] * 4,
        scratch_shapes=[pltpu.VMEM((8, 64, BLOCK), F32), dma(16)],
        compiler_params=PARAMS,
        cost_estimate=cost(0, 2 << 20),
    )(grad, got)


def replicas():
    me = lax.axis_index("rep")
    return [lax.rem(me + i, 4) for i in range(4)]


def pack_roots(roots, picks):
    def kernel(*refs):
        *outs, stage, sems = refs[len(roots) :]
        me, after, facing, before = replicas()
        run_copies([(refs[a].at[slot], stage.at[i]) for i, (a, slot) in enumerate(picks)], sems)
        pairs = []
        for i in range(4):
            down, up = outs[1 + i // 2 * 2 : 3 + i // 2 * 2]
            own = stage.at[i, :, at(me)]
            pairs += [(own, outs[0].at[i]), (own, down.at[i % 2]), (own, up.at[i % 2])]
            pairs.append((stage.at[i, :, at(after)], down.at[2 + i % 2]))
            pairs.append((stage.at[i, :, at(before)], up.at[2 + i % 2]))
            pairs.append((stage.at[i, :, at(facing)], (down, up)[i % 2].at[4]))
        run_copies(pairs, sems)

    return pl.pallas_call(
        kernel,
        name="pack_roots",
        in_specs=[HBM] * len(roots),
        out_specs=[HBM] * 5,
        out_shape=[array(4, BAND, BAND)] + [array(5, BAND, BAND)] * 4,
        scratch_shapes=[pltpu.VMEM((4, BAND, BLOCK), F32), dma(24)],
        compiler_params=SMALL,
        cost_estimate=cost(0, 2 << 20),
    )(*roots)


def follow(x, earlier):
    def kernel(*refs):
        pass

    return pl.pallas_call(
        kernel,
        name="follow",
        in_specs=[HBM] * 2,
        out_specs=HBM,
        out_shape=array(*x.shape),
        input_output_aliases={0: 0},
        compiler_params=PARAMS,
        cost_estimate=cost(0, 0),
    )(x, earlier)


def assemble(i, bands, above, below, across, whole):
    me, after, facing, before = replicas()

    def put(a, b, block):
        whole[at(a), at(b)] = block
        whole[at(b), at(a)] = block.T

    whole[at(me), :] = bands[i]
    for other in (after, facing, before):
        whole[at(other), at(me)] = bands[i, :, at(other)].T
    whole[at(after), at(after)] = above[i]
    whole[at(before), at(before)] = below[i]
    whole[at(facing), at(facing)] = across[i]
    put(after, facing, above[2 + i])
    put(before, facing, below[2 + i])
    if i:
        put(before, after, below[4])
    else:
        put(after, before, above[4])


def root_scratch():
    return [
        pltpu.VMEM((2, BAND, BLOCK), F32),
        pltpu.VMEM((5, BAND, BAND), F32),
        pltpu.VMEM((5, BAND, BAND), F32),
        pltpu.VMEM((2, BAND, BAND), F32),
        pltpu.VMEM((BLOCK, BLOCK), F32),
    ]


def apply_band(blocks, roots, picks, above, below, across, first):
    n = len(BANDED)

    def kernel(*refs):
        blocks, left, right, above_in, below_in, across_in, out = refs[:7]
        bands, above, below, across, whole, grad, right_v, result, sems = refs[7:]
        pairs = [(left.at[slot], bands.at[i]) for i, (_, slot) in enumerate(picks)]
        pairs += [(above_in, above), (below_in, below), (across_in.at[pl.ds(first, 2)], across)]
        pairs += [(right.at[slot], right_v.at[i]) for i, slot in enumerate(BANDED)]
        copies = copies_of(pairs, sems)
        loads = [
            pltpu.make_async_copy(blocks.at[:, pl.ds(i * BLOCK, BLOCK)], grad.at[i], sems.at[len(pairs) + i])
            for i in range(n)
        ]
        for copy in copies + loads:
            copy.start()
        for copy in copies:
            copy.wait()
        stores = []
        for i in range(n):
            assemble(i, bands, above, below, across, whole)
            left_root = split(whole[...])
            loads[i].wait()
            half = dot_beside(split(grad[i]), stacked(right_v[i]).T)
            columns = pl.ds(i * BAND, BAND)
            result[:, columns] = dot_beside(left_root, jnp.concatenate(split(half), axis=1))
            stores.append(pltpu.make_async_copy(result.at[:, columns], out.at[:, columns], sems.at[i]))
            stores[-1].start()
        for copy in stores:
            copy.wait()

    return pl.pallas_call(
        kernel,
        name="apply_band",
        in_specs=[HBM] * 6,
        out_specs=HBM,
        out_shape=array(BLOCK, n * BAND),
        scratch_shapes=root_scratch()
        + [
            pltpu.VMEM((n, BLOCK, BLOCK), F32),
            pltpu.VMEM((n, BAND, BLOCK), F32),
            pltpu.VMEM((BLOCK, n * BAND), F32),
            dma(9),
        ],
        compiler_params=PARAMS,
        cost_estimate=cost(n * 12 * BLOCK * BLOCK * BAND, n * 3 << 20),
    )(blocks, *roots, above, below, across)


def row_pairs(pieces, grad):
    y, _, _ = place()
    pairs = []
    for shift, piece in zip((0,) + SHIFTS, pieces):
        source = lax.rem(y + 4 - shift, 4)
        for core in range(2):
            rows = pl.ds(pl.multiple_of(source * BAND + core * 64, 64), 64)
            pairs.append((piece.at[core], grad.at[rows, :]))
    return pairs


def apply_whole(pieces, roots, picks, above, below, across, first):
    def kernel(*refs):
        pieces, refs = refs[:4], refs[4:]
        *roots, above_in, below_in, across_in, out, bands, above, below, across, whole, grad, result, sems = refs
        pairs = [(roots[a].at[slot], bands.at[i]) for i, (a, slot) in enumerate(picks)]
        pairs += [(above_in, above), (below_in, below), (across_in.at[pl.ds(first, 2)], across)]
        run_copies(pairs + row_pairs(pieces, grad), sems)
        assemble(1, bands, above, below, across, whole)
        half = split(dot3(split(grad[...]), split(whole[...]), ((1,), (0,))))
        assemble(0, bands, above, below, across, whole)
        stores = []
        for i in range(4):
            rows = pl.ds(i * BAND, BAND)
            result[rows, :] = dot_stacked(stacked(whole[rows, :]), half, ((1,), (0,)))
            stores.append(pltpu.make_async_copy(result.at[rows, :], out.at[rows, :], sems.at[i]))
            stores[-1].start()
        for copy in stores:
            copy.wait()

    return pl.pallas_call(
        kernel,
        name="apply_whole",
        in_specs=[HBM] * (7 + len(roots)),
        out_specs=HBM,
        out_shape=array(BLOCK, BLOCK),
        scratch_shapes=root_scratch()
        + [pltpu.VMEM((BLOCK, BLOCK), F32), pltpu.VMEM((BLOCK, BLOCK), F32), dma(13)],
        compiler_params=PARAMS,
        cost_estimate=pl.CostEstimate(flops=1 << 37, bytes_accessed=4 << 20, transcendentals=0),
    )(*pieces, *roots, above, below, across)


def grams(blocks, pieces, left_stat, right_stat):
    def kernel(blocks, *refs):
        *pieces, left, right, left_out, right_out, grad, stats, sems = refs
        me = lax.axis_index("rep")
        loads = []
        for slot in range(SLOTS):
            pairs = [(left.at[slot], stats.at[0, slot]), (right.at[slot], stats.at[1, slot])]
            if slot in BANDED:
                columns = pl.ds(BANDED.index(slot) * BLOCK, BLOCK)
                pairs.append((blocks.at[:, columns], grad.at[slot]))
            else:
                pairs += row_pairs(pieces, grad.at[slot])
            loads.append([pltpu.make_async_copy(a, b, sems.at[slot, i]) for i, (a, b) in enumerate(pairs)])
            for copy in loads[-1]:
                copy.start()
        stores = []
        weight = (1.0 - STAT_DECAY) / BLOCK
        for slot in range(SLOTS):
            for copy in loads[slot]:
                copy.wait()
            whole = split(grad[slot])
            rows = stacked(grad[slot, at(me), :])
            columns = stacked(grad[slot, :, at(me)].T)
            stats[0, slot] = STAT_DECAY * stats[0, slot] + weight * dot_stacked(rows, whole, ((1,), (1,)))
            stats[1, slot] = STAT_DECAY * stats[1, slot] + weight * dot_stacked(columns, whole, ((1,), (0,)))
            for i, out in enumerate((left_out, right_out)):
                stores.append(pltpu.make_async_copy(stats.at[i, slot], out.at[slot], sems.at[slot, 10 + i]))
                stores[-1].start()
        for copy in stores:
            copy.wait()

    return pl.pallas_call(
        kernel,
        name="grams",
        in_specs=[HBM] * 7,
        out_specs=[HBM] * 2,
        out_shape=[array(SLOTS, BAND, BLOCK)] * 2,
        scratch_shapes=[
            pltpu.VMEM((SLOTS, BLOCK, BLOCK), F32),
            pltpu.VMEM((2, SLOTS, BAND, BLOCK), F32),
            pltpu.SemaphoreType.DMA((SLOTS, 12)),
        ],
        compiler_params=SMALL,
        cost_estimate=cost(36 * BLOCK * BLOCK * BAND, 7 << 20),
    )(blocks, *pieces, left_stat, right_stat)


def join(pieces, filled):
    n = len(BANDED)

    def kernel(own, near, other, far, filled, out, own_v, rows, sems):
        _, core, me = place()
        load = pltpu.make_async_copy(own, own_v, sems.at[8, 0])
        load.start()
        stores = []
        for owner in range(8):
            target = out.at[:, pl.ds((SLOTS * owner + FILLED) * BLOCK, BLOCK)]
            stores.append(pltpu.make_async_copy(filled.at[owner], target, sems.at[owner, 0]))
            stores[-1].start()
        sources = (lax.rem(me + 3 - 2 * core, 4), lax.rem(me + 1 + 2 * core, 4), lax.rem(me + 2, 4), me)
        load.wait()
        for owner in range(8):
            for j, slot in enumerate(BANDED):
                for bands, source in zip((near, other, far, own_v), sources):
                    rows[owner, :, at(j * REPLICAS + source)] = bands[owner, :, j * BAND : (j + 1) * BAND]
                target = out.at[:, pl.ds((SLOTS * owner + slot) * BLOCK, BLOCK)]
                copy = pltpu.make_async_copy(rows.at[owner, :, pl.ds(j * BLOCK, BLOCK)], target, sems.at[owner, 1 + j])
                copy.start()
                stores.append(copy)
        for copy in stores:
            copy.wait()

    return pl.pallas_call(
        kernel,
        name="join",
        in_specs=[HBM] + [VMEM] * 4,
        out_specs=HBM,
        out_shape=array(64, 8 * OWNED),
        scratch_shapes=[
            pltpu.VMEM((8, 64, n * BAND), F32),
            pltpu.VMEM((8, 64, n * BLOCK), F32),
            pltpu.SemaphoreType.DMA((9, 1 + n)),
        ],
        compiler_params=SMALL,
        cost_estimate=cost(0, 6 << 20),
    )(*pieces, filled)


def shards(grad, left_stat, right_stat, left_root, right_root):
    groups = [[8 * g + p for p in range(8)] for g in range(8)]
    order = lax.optimization_barrier

    def exchange(x):
        return lax.all_to_all(x, "fsdp", 0, 0, axis_index_groups=groups, tiled=True)

    def along_y(x, distance):
        route = [(i, i - i % 8 + (i % 8 + 2 * distance) % 8) for i in range(64)]
        return lax.ppermute(x, "fsdp", route)

    def along_x(x, distance):
        return lax.ppermute(x, "rep", [(i, (i + distance) % REPLICAS) for i in range(REPLICAS)])

    def around(x, direction):
        ends = [(i, r, (r + (1 - 2 * (i % 2)) * direction) % REPLICAS) for i in range(64) for r in range(REPLICAS)]
        return lax.ppermute(x, ("fsdp", "rep"), [(REPLICAS * i + r, REPLICAS * i + t) for i, r, t in ends])

    def other_core(x):
        return lax.ppermute(x, "fsdp", [(i, i ^ 1) for i in range(64)])

    early, late = ((0, 0), (0, 1)), ((0, 2), (1, 2))
    roots = (left_root, right_root)
    dealt, roots = order((deal(grad), roots))
    blocks = exchange(dealt).reshape(BLOCK, len(BANDED) * BLOCK)
    across, *first, down, up = pack_roots(roots, early + late)
    across = along_x(across, 2)
    first = along_x(first[0], 3), along_x(first[1], 1)
    kept, *sent = pack(grad, other_core(deal_core(grad)))
    second = along_x(follow(down, across), 3), along_x(follow(up, across), 1)
    banded = apply_band(blocks, roots, early, *first, across, 0)
    pieces = [kept] + [along_y(x, d) for x, d in zip(sent, SHIFTS)]
    own = exchange(banded.reshape(8, 64, len(BANDED) * BAND))
    filled = apply_whole(pieces, roots, late, *second, across, 2)
    own, filled = order((own, filled))
    near = around(own, 1)
    filled = exchange(filled.reshape(8, 64, BLOCK))
    left_next, right_next = grams(blocks, pieces, left_stat, right_stat)
    out = join([own, near, around(own, -1), around(near, 1)], filled)
    return out, left_next, right_next


def solution(mesh):
    band = P("fsdp", "rep", None)
    return jax.shard_map(
        shards,
        mesh=mesh,
        in_specs=(P("fsdp", None), band, band, band, band),
        out_specs=(P("fsdp", None), band, band),
        check_vma=False,
    )
```
